128 devices in a mesh: row: 16 (over x_lo, y, core), col: 8 (over x_hi, z).
Axes of the slice: x: 4 (x_hi: 2, x_lo: 2; x = x_hi * 2 + x_lo), y: 4, z: 4, core: 2. Of those that a mesh axis runs over, the one named last changes fastest.
Arguments:
- features: bfloat16 [65536, 128], P(('col', 'row')), may hold values from -6 to 6
- weight: bfloat16 [128, 256], replicated, may hold values from -0.5 to 0.5
- degrees: int32 [65536], replicated, may hold values from 8 to 32
- tile_rows: int32 [16, 8, 768], P('row', 'col'), may hold values from 0 to 31, as said below
- tile_cols: int32 [16, 8, 768], P('row', 'col'), may hold values from 0 to 63, as said below
- tile_masks: int32 [16, 8, 768, 16, 128], P('row', 'col'), may hold values from 0 to 255, as said below
- cotangent: bfloat16 [65536, 256], P(('row', 'col')), may hold values from -10 to 10
Outputs:
- activated: bfloat16 [65536, 256], P(('row', 'col'))
- grad_features: float32 [65536, 128], P(('col', 'row'))
- grad_weight: float32 [128, 256], replicated
The draws below stay inside these ranges and needn't reach their ends.
Inputs may be any that keep to these rules, and one draw needn't show every extreme that they name: The degrees are those of the full graph, which is sparser than A; they are not A's row or column counts. `tile_rows`: each device's tiles fill its first slots; its remaining slots hold tile row 0 and tile column 0. At every grid row some device fills all 768 slots. Pairs may repeat, and repeated tiles add. `tile_cols`: empty slots hold 0. `tile_masks`: every word holds 8 bits; empty slots are all zero.
All inputs are finite; a program needn't handle non-finite values.
Results may differ from the reference program's by a relative error of at most 0.0049.
Values may be sent and summed in bfloat16 or wider, within the bound.
A program may use at most 128 MiB of HBM per device.

```python
import jax
import jax.numpy as jnp
from jax import lax

F_IN = 128
F_OUT = 256
NODES = 65536
ROW_TILES = 32
COL_TILES = 64
TILE_CAP = 768
N_ROW = 16
N_COL = 8


def slot_layout(key):
    key_full = jax.random.fold_in(key, 101)
    key_count = jax.random.fold_in(key, 102)
    full_col = jax.random.randint(key_full, (N_ROW, 1), 0, N_COL)
    other_count = jax.random.randint(key_count, (N_ROW, N_COL), TILE_CAP // 8, TILE_CAP // 2 + 1)
    counts = jnp.where(jnp.arange(N_COL)[None, :] == full_col, TILE_CAP, other_count)
    return jnp.arange(TILE_CAP)[None, None, :] < counts[:, :, None]


def draw_tile_rows(key, part):
    live_slot = slot_layout(key)
    key = jax.random.fold_in(key, 1)
    values = jax.random.randint(key, (N_ROW, N_COL, TILE_CAP), 0, ROW_TILES)
    return jnp.where(live_slot, values, 0).astype(jnp.int32)


def draw_tile_cols(key, part):
    live_slot = slot_layout(key)
    key = jax.random.fold_in(key, 2)
    values = jax.random.randint(key, (N_ROW, N_COL, TILE_CAP), 0, COL_TILES)
    return jnp.where(live_slot, values, 0).astype(jnp.int32)


def draw_tile_masks(key, part):
    live_slot = slot_layout(key)
    key = jax.random.fold_in(key, 3)
    shape = (N_ROW, N_COL, TILE_CAP, 16, 128)
    combined = jax.random.randint(jax.random.fold_in(key, 11), shape, 0, 256)
    combined = combined & jax.random.randint(jax.random.fold_in(key, 12), shape, 0, 256)
    combined = combined & jax.random.randint(jax.random.fold_in(key, 13), shape, 0, 256)
    combined = combined & jax.random.randint(jax.random.fold_in(key, 14), shape, 0, 256)
    return jnp.where(live_slot[:, :, :, None, None], combined, 0).astype(jnp.int32)


def draw_cotangent(key, part):
    key = jax.random.fold_in(key, 4)
    position = jnp.arange(NODES, dtype=jnp.float32) / NODES
    row_scale = 0.5 * jnp.power(3.0, position)[:, None]
    values = jnp.clip(jax.random.normal(key, (NODES, F_OUT), jnp.float32), -4.0, 4.0) * row_scale
    return values.astype(jnp.bfloat16)


def with_ends(array, key, low, high):
    dims = array.shape
    index_at = [jax.random.randint(jax.random.fold_in(key, axis), (), 0, dims[axis]) for axis in range(len(dims))]
    array = array.at[tuple(index_at)].set(low)
    longest = dims.index(max(dims))
    index_at[longest] = (index_at[longest] + 1) % dims[longest]
    return array.at[tuple(index_at)].set(high)


def level_of(key, extent, cuts, least, largest):
    def one(dim, shards_of):
        draws = jax.random.uniform(jax.random.fold_in(jax.random.fold_in(key, 6), dim), (shards_of,), jnp.float32, least / len(cuts), largest / len(cuts))
        return jnp.repeat(jnp.exp(draws), extent[dim] // shards_of).reshape((-1,) + (1,) * (len(extent) - dim - 1))

    gain = one(*cuts[0])
    for cut in cuts[1:]:
        gain = gain * one(*cut)
    return gain


def centred(own_key, dims, deviation, most, shards=(), kind=jnp.bfloat16):
    result = jax.random.normal(own_key, dims, jnp.float32) * deviation
    if len(shards) > 0:
        result = level_of(own_key, dims, shards, -0.22, 0.18) * result
    return jnp.clip(result, min=-most, max=most).astype(kind)


def setup_inputs(seed: int = 0) -> dict:
    seeds = jax.random.split(jax.random.key(seed), 8)
    features = centred(seeds[0], (NODES, F_IN), 1.0, 6.0, ((0, 128),))
    weight = centred(seeds[1], (F_IN, F_OUT), F_IN ** -0.5, 0.5)
    degrees = with_ends(jax.random.randint(seeds[2], (NODES,), 8, 33), jax.random.fold_in(seeds[2], 1), 8, 32).astype(jnp.int32)
    tile_rows = draw_tile_rows(jax.random.fold_in(seeds[7], 71), 0)
    tile_cols = draw_tile_cols(jax.random.fold_in(seeds[7], 71), 0)
    tile_masks = draw_tile_masks(jax.random.fold_in(seeds[7], 71), 0)
    cotangent = draw_cotangent(jax.random.fold_in(seeds[7], 71), 0)
    return {"features": features, "weight": weight, "degrees": degrees, "tile_rows": tile_rows, "tile_cols": tile_cols, "tile_masks": tile_masks, "cotangent": cotangent}


def unpack_tiles(mask_words):
    shifts = jnp.arange(8, dtype=jnp.int32)
    expanded = jnp.right_shift(mask_words[:, :, None, :], shifts[:, None]) & 1
    return expanded.reshape(mask_words.shape[0], 128, mask_words.shape[2])

def reference(features, weight, degrees, tile_rows, tile_cols, tile_masks, cotangent):
    inverse = lax.rsqrt(degrees.astype(jnp.float32))
    scaled = (features.astype(jnp.float32) * inverse[:, None]).astype(jnp.bfloat16)
    devices = N_ROW * N_COL
    grid_row = jnp.arange(devices, dtype=jnp.int32) // N_COL
    grid_col = jnp.arange(devices, dtype=jnp.int32) % N_COL
    global_rows = tile_rows.reshape(devices, TILE_CAP).astype(jnp.int32) + grid_row[:, None] * ROW_TILES
    global_cols = tile_cols.reshape(devices, TILE_CAP).astype(jnp.int32) + grid_col[:, None] * COL_TILES
    packed = tile_masks.reshape(devices, TILE_CAP, 16, 128)
    source_tiles = scaled.astype(jnp.float32).reshape(NODES // 128, 128, F_IN)

    def forward_step(totals, step_items):
        rows_here, cols_here, words_here = step_items
        tile_blocks = unpack_tiles(words_here).astype(jnp.float32)
        contrib = jnp.einsum('kji,kjf->kif', tile_blocks, source_tiles[cols_here])
        return (totals.at[rows_here].add(contrib), None)
    empty_sum = jnp.zeros((NODES // 128, 128, F_IN), jnp.float32)
    summed = lax.scan(forward_step, empty_sum, (global_rows, global_cols, packed))[0]
    aggregated = summed.reshape(NODES, F_IN) * inverse[:, None]
    weight_full = weight.astype(jnp.float32)
    pre_act = jnp.dot(aggregated, weight_full, precision=lax.Precision.HIGHEST)
    activated = jax.nn.elu(pre_act).astype(jnp.bfloat16)
    slope_factor = jnp.where(pre_act > 0, jnp.ones_like(pre_act), jnp.exp(jnp.minimum(pre_act, 0.0)))
    pre_grad = cotangent.astype(jnp.float32) * slope_factor
    grad_weight = jnp.dot(aggregated.T, pre_grad, precision=lax.Precision.HIGHEST) * NODES ** (-0.5)
    scaled_grad = (pre_grad * inverse[:, None]).astype(jnp.bfloat16)
    target_tiles = scaled_grad.astype(jnp.float32).reshape(NODES // 128, 128, F_OUT)

    def backward_step(totals, step_items):
        rows_here, cols_here, words_here = step_items
        tile_blocks = unpack_tiles(words_here).astype(jnp.float32)
        contrib = jnp.einsum('kji,kif->kjf', tile_blocks, target_tiles[rows_here])
        return (totals.at[cols_here].add(contrib), None)
    empty_back = jnp.zeros((NODES // 128, 128, F_OUT), jnp.float32)
    transposed = lax.scan(backward_step, empty_back, (global_rows, global_cols, packed))[0]
    transposed = transposed.reshape(NODES, F_OUT)
    grad_features = jnp.dot(transposed, weight_full.T, precision=lax.Precision.HIGHEST) * inverse[:, None]
    return (activated, grad_features, grad_weight)
```

```python
import functools

import jax
import jax.numpy as jnp
from jax import lax
from jax.experimental import pallas as pl
from jax.experimental.pallas import tpu as pltpu
from jax.sharding import PartitionSpec as P

F32 = jnp.float32
BF16 = jnp.bfloat16
I32 = jnp.int32
MESH = pl.DeviceIdType.MESH
VMEM = pltpu.VMEM
SLOTS = 1024
ROW_BITS = 5
COL_BITS = 6
CODE_BITS = ROW_BITS + COL_BITS
FWD_GROUP, FWD_UNROLL = 4, 4
BWD_GROUP, BWD_UNROLL = 4, 4
BIG = 48 * 1024 * 1024


def mm(a, b):
    return jnp.dot(a, b, preferred_element_type=F32)


def iota(shape, dim):
    return lax.broadcasted_iota(I32, shape, dim)


def split(x):
    hi = x.astype(BF16)
    return hi, (x - hi.astype(F32)).astype(BF16)


def greet(axis, count):
    me = lax.axis_index(axis)
    barrier = pltpu.get_barrier_semaphore()
    for step in range(1, count):
        peer = lax.rem(me + step, count)
        pl.semaphore_signal(barrier, inc=1, device_id={axis: peer}, device_id_type=MESH)
    pl.semaphore_wait(barrier, count - 1)


def order_list(keys, rows, cols, n_keys, group):
    cap = keys.shape[1]
    hot = iota((n_keys, cap), 0) == keys
    hot_f = hot.astype(F32)
    upper = (iota((cap, cap), 0) < iota((cap, cap), 1)).astype(F32).astype(BF16)
    rank = mm(hot_f.astype(BF16), upper)
    count = jnp.sum(hot_f, axis=1, keepdims=True)
    groups = jnp.floor((count + (group - 1)) * (1.0 / group))
    wide = jnp.broadcast_to(groups, (n_keys, 128)).astype(BF16)
    lower = (iota((n_keys, n_keys), 1) < iota((n_keys, n_keys), 0)).astype(F32).astype(BF16)
    base = mm(lower, wide)[:, :1] * group
    pos = jnp.sum(hot_f * (rank + base), axis=0, keepdims=True)
    place = (iota((SLOTS, cap), 0) == pos.astype(I32)).astype(F32).astype(BF16)
    which = iota((8, cap), 0)
    slot = iota((8, cap), 1)
    vals = jnp.where(
        which == 0,
        slot >> 4,
        jnp.where(
            which == 1,
            slot & 15,
            jnp.where(which == 2, cols, jnp.where(which == 3, rows, jnp.where(which == 4, 1, 0))),
        ),
    )
    vals = vals.astype(F32).astype(BF16)
    found = lax.dot_general(vals, place, (((1,), (1,)), ((), ())), preferred_element_type=F32)
    f = found.astype(I32)
    code = ((f[0:1] * 16 + f[1:2]) << CODE_BITS) | (f[2:3] << ROW_BITS) | f[3:4]
    code = jnp.where(f[4:5] > 0, code, cap << CODE_BITS)
    total = jnp.sum(groups, axis=0, keepdims=True).astype(I32)
    return jnp.where(iota((8, SLOTS), 0) == 0, code, total)


def gather_kernel(n, feat, deg, rows, cols, out, fwd_list, bwd_list, mine, send_sem, recv_sem, own_sem):
    me = lax.axis_index("row")
    lane = iota((128, 128), 1)
    perm = (iota((128, 128), 0) == ((lane & 15) * 8 + (lane >> 4))).astype(F32).astype(BF16)
    degrees = mm(deg[...].astype(F32).astype(BF16), perm)
    bucket = iota((1, 128), 1) >> 4
    shrink = jnp.zeros((1, 128), F32)
    for b in range(8):
        shrink = jnp.where(bucket == b, 2.0**-b, shrink)
    inverse = lax.rsqrt(degrees)
    for t in range(4):
        turned = lax.dot_general(
            feat[t * 128 : (t + 1) * 128, :], perm, (((0,), (0,)), ((), ())), preferred_element_type=F32
        )
        mine[t] = (turned * inverse[t : t + 1, :] * shrink).astype(BF16)
    greet("row", n)
    copies = []
    here = out.at[pl.ds(me * 4, 4)]
    for step in range(1, n):
        peer = lax.rem(me + step, n)
        copy = pltpu.make_async_remote_copy(
            src_ref=mine,
            dst_ref=here,
            send_sem=send_sem.at[step],
            recv_sem=recv_sem.at[step],
            device_id={"row": peer},
            device_id_type=MESH,
        )
        copy.start()
        copies.append(copy)
    own = pltpu.make_async_copy(mine, here, own_sem)
    own.start()
    r, c = rows[...], cols[...]
    fwd_list[...] = order_list(r, r, c, 1 << ROW_BITS, FWD_GROUP)
    bwd_list[...] = order_list(c, r, c, 1 << COL_BITS, BWD_GROUP)
    own.wait()
    for copy in copies:
        copy.wait()


def unpack(words):
    return [(words & (1 << b)).astype(F32).astype(BF16) for b in range(8)]


def load_masks(masks, held, sem):
    copy = pltpu.make_async_copy(masks, held.at[pl.ds(0, 768)], sem)
    copy.start()
    held[768] = jnp.zeros((16, 128), I32)
    return copy


def forward_kernel(codes, src, masks, out, held, acc, sem):
    copy = load_masks(masks, held, sem)
    acc[...] = jnp.zeros_like(acc)
    copy.wait()
    group, unroll = FWD_GROUP, FWD_UNROLL

    def body(i, carry):
        for u in range(unroll):
            at = (i * unroll + u) * group
            code = [codes[0, at + g] for g in range(group)]
            target = code[0] & ((1 << ROW_BITS) - 1)
            lhs = jnp.concatenate(
                [src[(k >> ROW_BITS) & ((1 << COL_BITS) - 1)] for k in code], axis=1
            )
            rhs = jnp.concatenate(
                [part for k in code for part in unpack(held[k >> CODE_BITS])], axis=0
            )
            acc[target] += mm(lhs, rhs)
        return carry

    lax.fori_loop(0, (codes[1, 0] + unroll - 1) // unroll, body, 0)
    out[...] = acc[...].astype(BF16)


def backward_kernel(codes, src, masks, out, held, acc, sem):
    copy = load_masks(masks, held, sem)
    acc[...] = jnp.zeros_like(acc)
    copy.wait()
    group, unroll = BWD_GROUP, BWD_UNROLL

    def body(i, carry):
        for u in range(unroll):
            at = (i * unroll + u) * group
            code = [codes[0, at + g] for g in range(group)]
            target = (code[0] >> ROW_BITS) & ((1 << COL_BITS) - 1)
            rhs = jnp.concatenate([src[k & ((1 << ROW_BITS) - 1)] for k in code], axis=0)
            lhs = jnp.concatenate(
                [jnp.concatenate(unpack(held[k >> CODE_BITS]), axis=0) for k in code], axis=1
            )
            acc[target] += mm(lhs, rhs)
        return carry

    lax.fori_loop(0, (codes[1, 0] + unroll - 1) // unroll, body, 0)
    out[...] = acc[...].astype(BF16)


def layer_kernel(n, scale, part, weight, deg, cot, act, out, gw, got, mine, s1, r1, s2, r2, own1, own2):
    me = lax.axis_index("col")
    greet("col", n)
    copies = []
    for step in range(1, n):
        peer = lax.rem(me + step, n)
        copy = pltpu.make_async_remote_copy(
            src_ref=part.at[pl.ds(peer * 4, 4)],
            dst_ref=got.at[step],
            send_sem=s1.at[step],
            recv_sem=r1.at[step],
            device_id={"col": peer},
            device_id_type=MESH,
        )
        copy.start()
        copies.append(copy)
    own = pltpu.make_async_copy(part.at[pl.ds(me * 4, 4)], got.at[0], own1)
    own.start()
    own.wait()
    for copy in copies:
        copy.wait()
    w = weight[...]
    inverse = lax.rsqrt(deg[...].astype(F32))
    total = jnp.zeros((128, 256), F32)
    for t in range(4):
        summed = got[0, t].astype(F32)
        for step in range(1, n):
            summed = summed + got[step, t].astype(F32)
        factor = jnp.broadcast_to(inverse[t : t + 1, :], (128, 128))
        agg_t = summed * factor
        factor = factor.T
        factor = jnp.concatenate([factor, factor], axis=1)
        t_hi, t_lo = split(agg_t)
        hi, lo = split(agg_t.T)
        pre = mm(hi, w) + mm(lo, w)
        slope = jnp.where(pre > 0, 1.0, jnp.exp(jnp.minimum(pre, 0.0)))
        rows = pl.ds(t * 128, 128)
        act[rows, :] = jnp.where(pre > 0, pre, slope - 1.0).astype(BF16)
        grad = cot[rows, :].astype(F32) * slope
        g_hi, g_lo = split(grad)
        total = total + (mm(t_hi, g_hi) + (mm(t_lo, g_hi) + mm(t_hi, g_lo)))
        scaled = (grad * factor).astype(BF16)
        mine[t] = lax.dot_general(
            scaled, w, (((1,), (1,)), ((), ())), preferred_element_type=F32
        ).astype(BF16)
    here = out.at[pl.ds(me * 4, 4)]
    copies = []
    for step in range(1, n):
        peer = lax.rem(me + step, n)
        copy = pltpu.make_async_remote_copy(
            src_ref=mine,
            dst_ref=here,
            send_sem=s2.at[step],
            recv_sem=r2.at[step],
            device_id={"col": peer},
            device_id_type=MESH,
        )
        copy.start()
        copies.append(copy)
    own = pltpu.make_async_copy(mine, here, own2)
    own.start()
    gw[...] = total * scale
    own.wait()
    for copy in copies:
        copy.wait()


def finish_kernel(
    n_row, n_col, part, deg, gw, out, gw_out, got, gw_got, gw_row, gw_col, gw_all,
    s1, r1, s2, r2, s3, r3, s4, r4, own_sem,
):
    row = lax.axis_index("row")
    col = lax.axis_index("col")
    barrier = pltpu.get_barrier_semaphore()
    for step in range(1, n_row):
        pl.semaphore_signal(
            barrier, inc=1, device_id={"row": lax.rem(row + step, n_row)}, device_id_type=MESH
        )
    for step in range(1, n_col):
        pl.semaphore_signal(
            barrier, inc=1, device_id={"col": lax.rem(col + step, n_col)}, device_id_type=MESH
        )
    pl.semaphore_wait(barrier, n_row + n_col - 2)

    def send(src, dst, sems, step, axis, me, count):
        copy = pltpu.make_async_remote_copy(
            src_ref=src,
            dst_ref=dst,
            send_sem=sems[0].at[step],
            recv_sem=sems[1].at[step],
            device_id={axis: lax.rem(me + step, count)},
            device_id_type=MESH,
        )
        copy.start()
        return copy

    weights = []
    for step in range(1, n_row):
        peer = lax.rem(row + step, n_row)
        weights.append(
            send(gw.at[pl.ds(peer * 8, 8)], gw_got.at[step], (s2, r2), step, "row", row, n_row)
        )
    main = []
    for step in range(1, n_row):
        peer = lax.rem(row + step, n_row)
        main.append(
            send(part.at[pl.ds(peer * 4, 4)], got.at[step], (s1, r1), step, "row", row, n_row)
        )
    own = pltpu.make_async_copy(part.at[pl.ds(row * 4, 4)], got.at[0], own_sem)
    own.start()
    for copy in weights:
        copy.wait()
    summed = gw[pl.ds(row * 8, 8), :]
    for step in range(1, n_row):
        summed = summed + gw_got[step]
    gw_row[...] = summed
    gw_col[pl.ds(col, 1)] = summed[None]
    weights = [
        send(gw_row, gw_col.at[col], (s3, r3), step, "col", col, n_col) for step in range(1, n_col)
    ]
    for copy in weights:
        copy.wait()
    summed = gw_col[0]
    for c in range(1, n_col):
        summed = summed + gw_col[c]
    mine = gw_all.at[pl.ds(row * 8, 8)]
    gw_all[pl.ds(row * 8, 8), :] = summed
    weights = [send(mine, mine, (s4, r4), step, "row", row, n_row) for step in range(1, n_row)]
    inverse = lax.rsqrt(deg[...].astype(F32))
    own.wait()
    for copy in main:
        copy.wait()
    for t in range(4):
        factor = jnp.broadcast_to(inverse[t : t + 1, :], (128, 128)).T
        for b in range(8):
            total = got[0, t, b * 16 : (b + 1) * 16, :].astype(F32)
            for step in range(1, n_row):
                total = total + got[step, t, b * 16 : (b + 1) * 16, :].astype(F32)
            out[pl.ds(t * 128 + b, 16, stride=8), :] = total * (2.0**-b)
        rows = pl.ds(t * 128, 128)
        out[rows, :] = out[rows, :] * factor
    for copy in weights:
        copy.wait()
    gw_out[...] = gw_all[...]


def spec(space=VMEM):
    return pl.BlockSpec(memory_space=space)


def shaped(shape, dtype):
    return jax.ShapeDtypeStruct(shape, dtype)


def remote_params(number):
    return pltpu.CompilerParams(
        collective_id=number, has_side_effects=True, vmem_limit_bytes=BIG
    )


def dma(count):
    return pltpu.SemaphoreType.DMA((count,))


def body(features, weight, degrees, tile_rows, tile_cols, tile_masks, cotangent):
    row = lax.axis_index("row")
    col = lax.axis_index("col")
    n_row = lax.axis_size("row")
    n_col = lax.axis_size("col")
    deg = degrees.reshape(n_row * n_col, 4, 128)
    deg_s = lax.dynamic_index_in_dim(deg, col * n_row + row, 0, False)
    deg_t = lax.dynamic_index_in_dim(deg, row * n_col + col, 0, False)
    rows = tile_rows.reshape(1, -1)
    cols = tile_cols.reshape(1, -1)
    masks = tile_masks.reshape(-1, 16, 128)
    hbm = spec(pl.ANY)
    n_rt, n_ct = 4 * n_col, 4 * n_row

    gathered, fwd_list, bwd_list = pl.pallas_call(
        functools.partial(gather_kernel, n_row),
        out_shape=(
            shaped((n_ct, 128, 128), BF16),
            shaped((8, SLOTS), I32),
            shaped((8, SLOTS), I32),
        ),
        in_specs=[spec()] * 4,
        out_specs=(hbm, spec(), spec()),
        scratch_shapes=[VMEM((4, 128, 128), BF16), dma(n_row), dma(n_row), pltpu.SemaphoreType.DMA],
        compiler_params=remote_params(0),
        name="gather_sources",
    )(features, deg_s, rows, cols)

    def product(kernel, codes, source, n_out, name):
        return pl.pallas_call(
            kernel,
            out_shape=shaped((n_out, 128, 128), BF16),
            in_specs=[spec(pltpu.SMEM), spec(), hbm],
            out_specs=spec(),
            scratch_shapes=[
                VMEM((776, 16, 128), I32),
                VMEM((n_out, 128, 128), F32),
                pltpu.SemaphoreType.DMA,
            ],
            compiler_params=pltpu.CompilerParams(vmem_limit_bytes=BIG),
            name=name,
        )(codes, source, masks)

    part = product(forward_kernel, fwd_list, gathered, n_rt, "tiles_forward")
    act, targets, gw = pl.pallas_call(
        functools.partial(layer_kernel, n_col, (512 * n_row * n_col) ** -0.5),
        out_shape=(
            shaped((512, 256), BF16),
            shaped((n_rt, 128, 128), BF16),
            shaped((128, 256), F32),
        ),
        in_specs=[hbm, spec(), spec(), spec()],
        out_specs=(spec(), hbm, spec()),
        scratch_shapes=[
            VMEM((n_col, 4, 128, 128), BF16),
            VMEM((4, 128, 128), BF16),
            dma(n_col),
            dma(n_col),
            dma(n_col),
            dma(n_col),
            pltpu.SemaphoreType.DMA,
            pltpu.SemaphoreType.DMA,
        ],
        compiler_params=remote_params(1),
        name="layer",
    )(part, weight, deg_t, cotangent)
    back = product(backward_kernel, bwd_list, targets, n_ct, "tiles_backward")
    grad_features, grad_weight = pl.pallas_call(
        functools.partial(finish_kernel, n_row, n_col),
        out_shape=(shaped((512, 128), F32), shaped((128, 256), F32)),
        in_specs=[hbm, spec(), spec()],
        out_specs=(spec(), spec()),
        scratch_shapes=[
            VMEM((n_row, 4, 128, 128), BF16),
            VMEM((n_row, 8, 256), F32),
            VMEM((8, 256), F32),
            VMEM((n_col, 8, 256), F32),
            VMEM((128, 256), F32),
            dma(n_row),
            dma(n_row),
            dma(n_row),
            dma(n_row),
            dma(n_col),
            dma(n_col),
            dma(n_row),
            dma(n_row),
            pltpu.SemaphoreType.DMA,
        ],
        compiler_params=remote_params(2),
        name="finish",
    )(back, deg_s, gw)
    return (act, grad_features, grad_weight)


def solution(mesh):
    in_specs = (
        P(("col", "row"), None),
        P(),
        P(),
        P("row", "col", None),
        P("row", "col", None),
        P("row", "col", None, None, None),
        P(("row", "col"), None),
    )
    out_specs = (P(("row", "col"), None), P(("col", "row"), None), P())
    return jax.shard_map(body, mesh=mesh, in_specs=in_specs, out_specs=out_specs, check_vma=False)
```

```python
import functools

import jax
import jax.numpy as jnp
from jax import lax
from jax.experimental import pallas as pl
from jax.experimental.pallas import tpu as pltpu
from jax.sharding import PartitionSpec as P

F32 = jnp.float32
BF16 = jnp.bfloat16
I32 = jnp.int32
MESH = pl.DeviceIdType.MESH
VMEM = pltpu.VMEM
SLOTS = 1024
ROW_BITS = 5
COL_BITS = 6
CODE_BITS = ROW_BITS + COL_BITS
FWD_GROUP, FWD_UNROLL = 4, 4
BWD_GROUP, BWD_UNROLL = 4, 4
BIG = 48 * 1024 * 1024


def mm(a, b):
    return jnp.dot(a, b, preferred_element_type=F32)


def iota(shape, dim):
    return lax.broadcasted_iota(I32, shape, dim)


def split(x):
    hi = x.astype(BF16)
    return hi, (x - hi.astype(F32)).astype(BF16)


class Place:
    def __init__(self, axis):
        self.axis = axis
        me = lax.axis_index(axis)
        if axis == "row":
            self.core = lax.rem(me, 2)
            chip = me // 2
        else:
            self.core = None
            chip = me
        self.p, self.q = chip // 4, lax.rem(chip, 4)

    def chip(self, name):
        p = 1 - self.p if name[0] == "x" else self.p
        turn = {"": 0, "m": 3, "p": 1, "2": 2}[name[1:]]
        return p * 4 + lax.rem(self.q + turn, 4)

    def index(self, name):
        chip = self.chip(name)
        return chip if self.core is None else chip * 2 + self.core

    def device(self, name):
        if name == "twin":
            return {self.axis: (self.p * 4 + self.q) * 2 + 1 - self.core}
        return {self.axis: self.index(name)}

    def partners(self):
        return ["x", "om", "op"] + ([] if self.core is None else ["twin"])


def send(src, dst, sems, i, device):
    copy = pltpu.make_async_remote_copy(
        src_ref=src,
        dst_ref=dst,
        send_sem=sems[0].at[i],
        recv_sem=sems[1].at[i],
        device_id=device,
        device_id_type=MESH,
    )
    copy.start()
    return copy


def landed(ref, sem):
    pltpu.make_async_copy(ref, ref, sem).wait()


def greet(place):
    barrier = pltpu.get_barrier_semaphore()
    names = place.partners()
    for name in names:
        pl.semaphore_signal(
            barrier, inc=1, device_id=place.device(name), device_id_type=MESH
        )
    pl.semaphore_wait(barrier, len(names))


PIECES = [
    ("x", 0, 4), ("om", 0, 4), ("op", 0, 4), ("o2", 0, 2), ("o2", 2, 2),
    ("xm", 0, 4), ("xp", 0, 4), ("x2", 0, 2), ("x2", 2, 2), ("o", 0, 4),
]


def spread(place, mine, out, sems, twin_sems):
    sent = []

    def region(i):
        name, first, tiles = PIECES[i]
        return out.at[pl.ds(place.index(name) * 4 + first, tiles)]

    def pass_on(i, to, dst, src):
        sent.append(send(src, dst, sems, i, place.device(to)))

    def twin(i, src):
        if place.core is not None:
            sent.append(send(src, region(i), twin_sems, i, place.device("twin")))

    here = region(9)
    for i, to in ((0, "x"), (1, "op"), (2, "om")):
        pass_on(i, to, here, mine)
    twin(9, mine)

    def forward(i, targets):
        ref = region(i)
        landed(ref, sems[1].at[i])
        for j, to in targets:
            pass_on(j, to, ref, ref)
        twin(i, ref)

    def forward_half(i, j, to):
        name, _, tiles = PIECES[i]
        landed(region(i), sems[1].at[i])
        half = out.at[pl.ds(place.index(name) * 4 + PIECES[j][1], 2)]
        pass_on(j, to, half, half)
        twin(i, region(i))

    def finish():
        forward(0, ((5, "op"), (6, "om")))
        forward_half(1, 3, "op")
        forward_half(2, 4, "om")
        forward(3, ((7, "x"),))
        forward(4, ((8, "x"),))
        for i in (5, 6, 7, 8):
            forward(i, ())
        if place.core is not None:
            for i in range(10):
                name, first, tiles = PIECES[i]
                index = place.chip(name) * 2 + 1 - place.core
                landed(out.at[pl.ds(index * 4 + first, tiles)], twin_sems[1].at[i])
        for copy in sent:
            copy.wait_send()

    return finish


def gather_up(place, first, value, staged, got, sems):
    sent = []

    def go(i, src, dst, to):
        sent.append(send(src, dst, sems, i, place.device(to)))

    def stage(name, slot, tiles, *refs):
        for t in tiles:
            total = value(name, t)
            for ref in refs:
                total = total + ref[t].astype(F32)
            staged[slot, t] = total.astype(BF16)

    go(0, first("x2"), got.at[0], "x")
    go(1, first("xm"), got.at[1], "om")
    go(2, first("xp"), got.at[2], "op")
    yield
    landed(got.at[0], sems[1].at[0])
    stage("o2", 3, range(4), got.at[0])
    go(3, staged.at[3, pl.ds(0, 2)], got.at[3, pl.ds(0, 2)], "om")
    go(4, staged.at[3, pl.ds(2, 2)], got.at[3, pl.ds(2, 2)], "op")
    landed(got.at[1], sems[1].at[1])
    landed(got.at[2], sems[1].at[2])
    stage("x", 4, range(4), got.at[1], got.at[2])
    go(5, staged.at[4], got.at[4], "x")
    landed(got.at[3, pl.ds(0, 2)], sems[1].at[3])
    stage("om", 5, (0, 1), got.at[3])
    stage("om", 5, (2, 3))
    go(6, staged.at[5], got.at[5], "om")
    landed(got.at[3, pl.ds(2, 2)], sems[1].at[4])
    stage("op", 6, (2, 3), got.at[3])
    stage("op", 6, (0, 1))
    go(7, staged.at[6], got.at[6], "op")
    yield
    for i in (4, 5, 6):
        landed(got.at[i], sems[1].at[i + 1])
    for copy in sent:
        copy.wait_send()


def gathered_tile(value, got, t):
    total = value("o", t)
    for i in (4, 5, 6):
        total = total + got[i, t].astype(F32)
    return total


def order_list(keys, rows, cols, n_keys, group):
    cap = keys.shape[1]
    hot = iota((n_keys, cap), 0) == keys
    hot_f = hot.astype(F32)
    upper = (iota((cap, cap), 0) < iota((cap, cap), 1)).astype(F32).astype(BF16)
    rank = mm(hot_f.astype(BF16), upper)
    count = jnp.sum(hot_f, axis=1, keepdims=True)
    groups = jnp.floor((count + (group - 1)) * (1.0 / group))
    wide = jnp.broadcast_to(groups, (n_keys, 128)).astype(BF16)
    lower = (iota((n_keys, n_keys), 1) < iota((n_keys, n_keys), 0)).astype(F32).astype(BF16)
    base = mm(lower, wide)[:, :1] * group
    pos = jnp.sum(hot_f * (rank + base), axis=0, keepdims=True)
    place = (iota((SLOTS, cap), 0) == pos.astype(I32)).astype(F32).astype(BF16)
    which = iota((8, cap), 0)
    slot = iota((8, cap), 1)
    vals = jnp.where(
        which == 0,
        slot >> 4,
        jnp.where(
            which == 1,
            slot & 15,
            jnp.where(which == 2, cols, jnp.where(which == 3, rows, jnp.where(which == 4, 1, 0))),
        ),
    )
    vals = vals.astype(F32).astype(BF16)
    found = lax.dot_general(vals, place, (((1,), (1,)), ((), ())), preferred_element_type=F32)
    f = found.astype(I32)
    code = ((f[0:1] * 16 + f[1:2]) << CODE_BITS) | (f[2:3] << ROW_BITS) | f[3:4]
    code = jnp.where(f[4:5] > 0, code, cap << CODE_BITS)
    total = jnp.sum(groups, axis=0, keepdims=True).astype(I32)
    return jnp.where(iota((8, SLOTS), 0) == 0, code, total)


def gather_kernel(
    feat, deg, rows, cols, out, fwd_list, bwd_list, mine, s1, r1, s2, r2, own_sem
):
    place = Place("row")
    lane = iota((128, 128), 1)
    perm = (iota((128, 128), 0) == ((lane & 15) * 8 + (lane >> 4))).astype(F32).astype(BF16)
    degrees = mm(deg[...].astype(F32).astype(BF16), perm)
    bucket = iota((1, 128), 1) >> 4
    shrink = jnp.zeros((1, 128), F32)
    for b in range(8):
        shrink = jnp.where(bucket == b, 2.0**-b, shrink)
    inverse = lax.rsqrt(degrees)
    for t in range(4):
        turned = lax.dot_general(
            feat[t * 128 : (t + 1) * 128, :], perm, (((0,), (0,)), ((), ())), preferred_element_type=F32
        )
        mine[t] = (turned * inverse[t : t + 1, :] * shrink).astype(BF16)
    greet(place)
    finish = spread(place, mine, out, (s1, r1), (s2, r2))
    own = pltpu.make_async_copy(mine, out.at[pl.ds(place.index("o") * 4, 4)], own_sem)
    own.start()
    r, c = rows[...], cols[...]
    fwd_list[...] = order_list(r, r, c, 1 << ROW_BITS, FWD_GROUP)
    bwd_list[...] = order_list(c, r, c, 1 << COL_BITS, BWD_GROUP)
    own.wait()
    finish()


def unpack(words):
    return [(words & (1 << b)).astype(F32).astype(BF16) for b in range(8)]


def load_masks(masks, held, sem):
    copy = pltpu.make_async_copy(masks, held.at[pl.ds(0, 768)], sem)
    copy.start()
    held[768] = jnp.zeros((16, 128), I32)
    return copy


def forward_kernel(codes, src, masks, out, held, acc, sem):
    copy = load_masks(masks, held, sem)
    acc[...] = jnp.zeros_like(acc)
    copy.wait()
    group, unroll = FWD_GROUP, FWD_UNROLL

    def body(i, carry):
        for u in range(unroll):
            at = (i * unroll + u) * group
            code = [codes[0, at + g] for g in range(group)]
            target = code[0] & ((1 << ROW_BITS) - 1)
            lhs = jnp.concatenate(
                [src[(k >> ROW_BITS) & ((1 << COL_BITS) - 1)] for k in code], axis=1
            )
            rhs = jnp.concatenate(
                [part for k in code for part in unpack(held[k >> CODE_BITS])], axis=0
            )
            acc[target] += mm(lhs, rhs)
        return carry

    lax.fori_loop(0, (codes[1, 0] + unroll - 1) // unroll, body, 0)
    out[...] = acc[...].astype(BF16)


def backward_kernel(codes, src, masks, out, held, acc, sem):
    copy = load_masks(masks, held, sem)
    acc[...] = jnp.zeros_like(acc)
    copy.wait()
    group, unroll = BWD_GROUP, BWD_UNROLL

    def body(i, carry):
        for u in range(unroll):
            at = (i * unroll + u) * group
            code = [codes[0, at + g] for g in range(group)]
            target = (code[0] >> ROW_BITS) & ((1 << COL_BITS) - 1)
            rhs = jnp.concatenate([src[k & ((1 << ROW_BITS) - 1)] for k in code], axis=0)
            lhs = jnp.concatenate(
                [jnp.concatenate(unpack(held[k >> CODE_BITS]), axis=0) for k in code], axis=1
            )
            acc[target] += mm(lhs, rhs)
        return carry

    lax.fori_loop(0, (codes[1, 0] + unroll - 1) // unroll, body, 0)
    out[...] = acc[...].astype(BF16)


def layer_kernel(
    scale, part, weight, deg, cot, act, out, gw, held, staged, got, mine, s1, r1, s2, r2, own1, own2
):
    place = Place("col")
    own = pltpu.make_async_copy(part, held, own1)
    own.start()
    greet(place)

    def value(name, t):
        return held[place.chip(name), t].astype(F32)

    steps = gather_up(place, lambda name: part.at[place.chip(name)], value, staged, got, (s1, r1))
    next(steps)
    own.wait()
    for _ in steps:
        pass
    w = weight[...]
    inverse = lax.rsqrt(deg[...].astype(F32))
    total = jnp.zeros((128, 256), F32)
    for t in range(4):
        summed = gathered_tile(value, got, t)
        factor = jnp.broadcast_to(inverse[t : t + 1, :], (128, 128))
        agg_t = summed * factor
        factor = factor.T
        factor = jnp.concatenate([factor, factor], axis=1)
        t_hi, t_lo = split(agg_t)
        hi, lo = split(agg_t.T)
        pre = mm(hi, w) + mm(lo, w)
        slope = jnp.where(pre > 0, 1.0, jnp.exp(jnp.minimum(pre, 0.0)))
        rows = pl.ds(t * 128, 128)
        act[rows, :] = jnp.where(pre > 0, pre, slope - 1.0).astype(BF16)
        grad = cot[rows, :].astype(F32) * slope
        g_hi, g_lo = split(grad)
        total = total + (mm(t_hi, g_hi) + (mm(t_lo, g_hi) + mm(t_hi, g_lo)))
        scaled = (grad * factor).astype(BF16)
        mine[t] = lax.dot_general(
            scaled, w, (((1,), (1,)), ((), ())), preferred_element_type=F32
        ).astype(BF16)
    finish = spread(place, mine, out, (s2, r2), None)
    own = pltpu.make_async_copy(mine, out.at[pl.ds(place.index("o") * 4, 4)], own2)
    own.start()
    gw[...] = total * scale
    own.wait()
    finish()


def finish_kernel(
    n_row, n_col, part, deg, gw, out, gw_out, held, from_twin, staged, got, gw_got, gw_row, gw_col, gw_all,
    s0, r0, s1, r1, s2, r2, s3, r3, s4, r4, own_sem,
):
    place = Place("row")
    row = lax.axis_index("row")
    col = lax.axis_index("col")
    own = pltpu.make_async_copy(part.at[:, place.core], held, own_sem)
    own.start()
    barrier = pltpu.get_barrier_semaphore()

    def row_peer(step):
        return {"row": lax.rem(row + step, n_row)}

    def col_peer(step):
        return {"col": lax.rem(col + step, n_col)}

    for step in range(1, n_row):
        pl.semaphore_signal(barrier, inc=1, device_id=row_peer(step), device_id_type=MESH)
    for step in range(1, n_col):
        pl.semaphore_signal(barrier, inc=1, device_id=col_peer(step), device_id_type=MESH)
    pl.semaphore_wait(barrier, n_row + n_col - 2)

    order = ["x2", "xm", "xp", "o2", "x", "om", "op", "o"]
    twins = [
        send(
            part.at[place.chip(name), 1 - place.core],
            from_twin.at[k],
            (s0, r0),
            k,
            place.device("twin"),
        )
        for k, name in enumerate(order)
    ]
    weights = [
        send(
            gw.at[pl.ds(lax.rem(row + step, n_row) * 8, 8)],
            gw_got.at[step],
            (s2, r2),
            step,
            row_peer(step),
        )
        for step in range(1, n_row)
    ]
    own.wait()

    def value(name, t):
        k = order.index(name)
        return held[place.chip(name), t].astype(F32) + from_twin[k, t].astype(F32)

    def first(name):
        k = order.index(name)
        landed(from_twin.at[k], r0.at[k])
        for t in range(4):
            staged[k, t] = value(name, t).astype(BF16)
        return staged.at[k]

    steps = gather_up(place, first, value, staged, got, (s1, r1))
    next(steps)
    for k in range(3, 8):
        landed(from_twin.at[k], r0.at[k])
    for copy in weights:
        copy.wait()
    summed = gw[pl.ds(row * 8, 8), :]
    for step in range(1, n_row):
        summed = summed + gw_got[step]
    gw_row[...] = summed
    gw_col[pl.ds(col, 1)] = summed[None]
    weights = [
        send(gw_row, gw_col.at[col], (s3, r3), step, col_peer(step)) for step in range(1, n_col)
    ]
    next(steps)
    for copy in weights:
        copy.wait_send()
    for step in range(1, n_col):
        landed(gw_col.at[lax.rem(col + n_col - step, n_col)], r3.at[step])
    summed = gw_col[0]
    for c in range(1, n_col):
        summed = summed + gw_col[c]
    mine = gw_all.at[pl.ds(row * 8, 8)]
    gw_all[pl.ds(row * 8, 8), :] = summed
    weights = [send(mine, mine, (s4, r4), step, row_peer(step)) for step in range(1, n_row)]
    inverse = lax.rsqrt(deg[...].astype(F32))
    for _ in steps:
        pass
    lane_b = iota((128, 128), 0) >> 4
    grow = jnp.zeros((128, 128), F32)
    for b in range(8):
        grow = jnp.where(lane_b == b, 2.0**-b, grow)
    for t in range(4):
        factor = jnp.broadcast_to(inverse[t : t + 1, :], (128, 128)).T
        total = gathered_tile(value, got, t) * grow
        for b in range(8):
            out[pl.ds(t * 128 + b, 16, stride=8), :] = total[b * 16 : (b + 1) * 16, :]
        rows = pl.ds(t * 128, 128)
        out[rows, :] = out[rows, :] * factor
    for copy in twins:
        copy.wait_send()
    for copy in weights:
        copy.wait()
    gw_out[...] = gw_all[...]


def spec(space=VMEM):
    return pl.BlockSpec(memory_space=space)


def shaped(shape, dtype):
    return jax.ShapeDtypeStruct(shape, dtype)


def remote_params(number):
    return pltpu.CompilerParams(
        collective_id=number, has_side_effects=True, vmem_limit_bytes=BIG
    )


def dma(count):
    return pltpu.SemaphoreType.DMA((count,))


def body(features, weight, degrees, tile_rows, tile_cols, tile_masks, cotangent):
    row = lax.axis_index("row")
    col = lax.axis_index("col")
    n_row = lax.axis_size("row")
    n_col = lax.axis_size("col")
    deg = degrees.reshape(n_row * n_col, 4, 128)
    deg_s = lax.dynamic_index_in_dim(deg, col * n_row + row, 0, False)
    deg_t = lax.dynamic_index_in_dim(deg, row * n_col + col, 0, False)
    rows = tile_rows.reshape(1, -1)
    cols = tile_cols.reshape(1, -1)
    masks = tile_masks.reshape(-1, 16, 128)
    hbm = spec(pl.ANY)
    n_rt, n_ct = 4 * n_col, 4 * n_row

    gathered, fwd_list, bwd_list = pl.pallas_call(
        gather_kernel,
        out_shape=(
            shaped((n_ct, 128, 128), BF16),
            shaped((8, SLOTS), I32),
            shaped((8, SLOTS), I32),
        ),
        in_specs=[spec()] * 4,
        out_specs=(hbm, spec(), spec()),
        scratch_shapes=[VMEM((4, 128, 128), BF16), dma(10), dma(10), dma(10), dma(10), pltpu.SemaphoreType.DMA],
        compiler_params=remote_params(0),
        name="gather_sources",
    )(features, deg_s, rows, cols)

    def product(kernel, codes, source, n_out, name):
        return pl.pallas_call(
            kernel,
            out_shape=shaped((n_out, 128, 128), BF16),
            in_specs=[spec(pltpu.SMEM), spec(), hbm],
            out_specs=spec(),
            scratch_shapes=[
                VMEM((776, 16, 128), I32),
                VMEM((n_out, 128, 128), F32),
                pltpu.SemaphoreType.DMA,
            ],
            compiler_params=pltpu.CompilerParams(vmem_limit_bytes=BIG),
            name=name,
        )(codes, source, masks)

    part = product(forward_kernel, fwd_list, gathered, n_rt, "tiles_forward")
    act, targets, gw = pl.pallas_call(
        functools.partial(layer_kernel, (512 * n_row * n_col) ** -0.5),
        out_shape=(
            shaped((512, 256), BF16),
            shaped((n_rt, 128, 128), BF16),
            shaped((128, 256), F32),
        ),
        in_specs=[hbm, spec(), spec(), spec()],
        out_specs=(spec(), hbm, spec()),
        scratch_shapes=[
            VMEM((8, 4, 128, 128), BF16),
            VMEM((8, 4, 128, 128), BF16),
            VMEM((7, 4, 128, 128), BF16),
            VMEM((4, 128, 128), BF16),
            dma(8),
            dma(8),
            dma(10),
            dma(10),
            pltpu.SemaphoreType.DMA,
            pltpu.SemaphoreType.DMA,
        ],
        compiler_params=remote_params(1),
        name="layer",
    )(part.reshape(8, 4, 128, 128), weight, deg_t, cotangent)
    back = product(backward_kernel, bwd_list, targets, n_ct, "tiles_backward")
    grad_features, grad_weight = pl.pallas_call(
        functools.partial(finish_kernel, n_row, n_col),
        out_shape=(shaped((512, 128), F32), shaped((128, 256), F32)),
        in_specs=[hbm, spec(), spec()],
        out_specs=(spec(), spec()),
        scratch_shapes=[
            VMEM((8, 4, 128, 128), BF16),
            VMEM((8, 4, 128, 128), BF16),
            VMEM((8, 4, 128, 128), BF16),
            VMEM((7, 4, 128, 128), BF16),
            VMEM((n_row, 8, 256), F32),
            VMEM((8, 256), F32),
            VMEM((n_col, 8, 256), F32),
            VMEM((128, 256), F32),
            dma(8),
            dma(8),
            dma(8),
            dma(8),
            dma(n_row),
            dma(n_row),
            dma(n_col),
            dma(n_col),
            dma(n_row),
            dma(n_row),
            pltpu.SemaphoreType.DMA,
        ],
        compiler_params=remote_params(2),
        name="finish",
    )(back.reshape(8, 2, 4, 128, 128), deg_s, gw)
    return (act, grad_features, grad_weight)


def solution(mesh):
    in_specs = (
        P(("col", "row"), None),
        P(),
        P(),
        P("row", "col", None),
        P("row", "col", None),
        P("row", "col", None, None, None),
        P(("row", "col"), None),
    )
    out_specs = (P(("row", "col"), None), P(("col", "row"), None), P())
    return jax.shard_map(body, mesh=mesh, in_specs=in_specs, out_specs=out_specs, check_vma=False)
```

```python
import functools
import itertools

import jax
import jax.numpy as jnp
from jax import lax
from jax.experimental import pallas as pl
from jax.experimental.pallas import tpu as pltpu
from jax.sharding import PartitionSpec as P

F32 = jnp.float32
BF16 = jnp.bfloat16
I32 = jnp.int32
MESH = pl.DeviceIdType.MESH
VMEM = pltpu.VMEM
SLOTS = 1024
ROW_BITS = 5
COL_BITS = 6
CODE_BITS = ROW_BITS + COL_BITS
FRESH = 24
GROUP, UNROLL = 4, 16
FWD_ROUNDS, BWD_ROUNDS = 14, 15
EMPTY = BWD_ROUNDS * UNROLL
BIG = 56 * 1024 * 1024


def mm(a, b):
    return jnp.dot(a, b, preferred_element_type=F32)


def iota(shape, dim):
    return lax.broadcasted_iota(I32, shape, dim)


def split(x):
    hi = x.astype(BF16)
    return hi, (x - hi.astype(F32)).astype(BF16)


class Place:
    def __init__(self, axis):
        self.axis = axis
        me = lax.axis_index(axis)
        if axis == "row":
            self.core = lax.rem(me, 2)
            chip = me // 2
        else:
            self.core = None
            chip = me
        self.p, self.q = chip // 4, lax.rem(chip, 4)

    def chip(self, name):
        p = 1 - self.p if name[0] == "x" else self.p
        turn = {"": 0, "m": 3, "p": 1, "2": 2}[name[1:]]
        return p * 4 + lax.rem(self.q + turn, 4)

    def index(self, name):
        chip = self.chip(name)
        return chip if self.core is None else chip * 2 + self.core

    def device(self, name):
        if name == "twin":
            return {self.axis: (self.p * 4 + self.q) * 2 + 1 - self.core}
        return {self.axis: self.index(name)}

    def partners(self):
        return ["x", "om", "op"] + ([] if self.core is None else ["twin"])


def send(src, dst, sems, i, device):
    copy = pltpu.make_async_remote_copy(
        src_ref=src,
        dst_ref=dst,
        send_sem=sems[0].at[i],
        recv_sem=sems[1].at[i],
        device_id=device,
        device_id_type=MESH,
    )
    copy.start()
    return copy


def landed(ref, sem):
    pltpu.make_async_copy(ref, ref, sem).wait()


class Place:
    def __init__(self, axis):
        self.axis = axis
        me = lax.axis_index(axis)
        if axis == "row":
            self.core = lax.rem(me, 2)
            chip = me // 2
        else:
            self.core = None
            chip = me
        self.p, self.q = chip // 4, lax.rem(chip, 4)

    def chip(self, name):
        p = 1 - self.p if name[0] == "x" else self.p
        turn = {"": 0, "m": 3, "p": 1, "2": 2}[name[1:]]
        return p * 4 + lax.rem(self.q + turn, 4)

    def index(self, name):
        chip = self.chip(name)
        return chip if self.core is None else chip * 2 + self.core

    def device(self, name):
        if name == "twin":
            return {self.axis: (self.p * 4 + self.q) * 2 + 1 - self.core}
        return {self.axis: self.index(name)}

def send(src, dst, sems, i, device):
    copy = pltpu.make_async_remote_copy(
        src_ref=src,
        dst_ref=dst,
        send_sem=sems[0].at[i],
        recv_sem=sems[1].at[i],
        device_id=device,
        device_id_type=MESH,
    )
    copy.start()
    return copy


def landed(ref, sem):
    pltpu.make_async_copy(ref, ref, sem).wait()


def together(*parts):
    for _ in itertools.zip_longest(*parts):
        pass


PIECES = [
    ("x", 0, 2), ("om", 0, 2), ("op", 0, 2), ("o2", 0, 1), ("o2", 1, 1),
    ("xm", 0, 2), ("xp", 0, 2), ("x2", 0, 1), ("x2", 1, 1), ("o", 0, 2),
]


def spread(place, mine, out, sems, twin_sems, chunk, sent):
    low = 10 * chunk

    def part(index, first, tiles):
        return out.at[pl.ds(index * 4 + 2 * chunk + first, tiles)]

    def region(i):
        name, first, tiles = PIECES[i]
        return part(place.index(name), first, tiles)

    def pass_on(i, to, dst, src):
        sent.append(send(src, dst, sems, low + i, place.device(to)))

    def twin(i, src):
        if place.core is not None:
            sent.append(send(src, region(i), twin_sems, low + i, place.device("twin")))

    own = mine.at[pl.ds(2 * chunk, 2)]
    for i, to in ((0, "x"), (1, "op"), (2, "om")):
        pass_on(i, to, region(9), own)
    twin(9, own)
    yield

    def forward(i, targets):
        ref = region(i)
        landed(ref, sems[1].at[low + i])
        for j, to in targets:
            pass_on(j, to, ref, ref)
        twin(i, ref)

    def forward_half(i, j, to):
        landed(region(i), sems[1].at[low + i])
        half = part(place.index(PIECES[i][0]), PIECES[j][1], 1)
        pass_on(j, to, half, half)
        twin(i, region(i))

    forward(0, ((5, "op"), (6, "om")))
    yield
    forward_half(1, 3, "op")
    yield
    forward_half(2, 4, "om")
    yield
    forward(3, ((7, "x"),))
    yield
    forward(4, ((8, "x"),))
    yield
    for i in (5, 6, 7, 8):
        forward(i, ())
        yield
    if place.core is not None:
        for i in range(10):
            name, first, tiles = PIECES[i]
            ref = part(place.chip(name) * 2 + 1 - place.core, first, tiles)
            landed(ref, twin_sems[1].at[low + i])


def gather_up(place, ready, value, staged, got, sems, chunk, sent):
    low = 8 * chunk
    t0, t1 = 2 * chunk, 2 * chunk + 1
    both = pl.ds(t0, 2)

    def go(i, slot, into, at, to):
        src, dst = staged.at[slot, at], got.at[into, at]
        sent.append(send(src, dst, sems, low + i, place.device(to)))

    def wait(i, into, at=both):
        landed(got.at[into, at], sems[1].at[low + i])

    def stage(name, slot, tiles, *slots):
        for t in tiles:
            total = value(name, t)
            for k in slots:
                total = total + got[k, t].astype(F32)
            staged[slot, t] = total.astype(BF16)

    for i, name, to in ((0, "x2", "x"), (1, "xm", "om"), (2, "xp", "op")):
        ready(name)
        stage(name, i, (t0, t1))
        go(i, i, i, both, to)
    yield
    wait(0, 0)
    ready("o2")
    stage("o2", 3, (t0, t1), 0)
    go(3, 3, 3, pl.ds(t0, 1), "om")
    go(4, 3, 3, pl.ds(t1, 1), "op")
    yield
    wait(1, 1)
    wait(2, 2)
    ready("x")
    stage("x", 4, (t0, t1), 1, 2)
    go(5, 4, 4, both, "x")
    yield
    ready("om")
    wait(3, 3, pl.ds(t0, 1))
    stage("om", 5, (t0,), 3)
    stage("om", 5, (t1,))
    go(6, 5, 5, both, "om")
    yield
    ready("op")
    wait(4, 3, pl.ds(t1, 1))
    stage("op", 6, (t1,), 3)
    stage("op", 6, (t0,))
    go(7, 6, 6, both, "op")
    yield
    ready("o")
    for i in (4, 5, 6):
        wait(i + 1, i)
    yield


def gathered_tile(value, got, t):
    total = value("o", t)
    for i in (4, 5, 6):
        total = total + got[i, t].astype(F32)
    return total


def order_list(keys, rows, cols, n_keys, group):
    cap = keys.shape[1]
    hot = iota((n_keys, cap), 0) == keys
    hot_f = hot.astype(F32)
    upper = (iota((cap, cap), 0) < iota((cap, cap), 1)).astype(F32).astype(BF16)
    rank = mm(hot_f.astype(BF16), upper)
    count = jnp.sum(hot_f, axis=1, keepdims=True)
    groups = jnp.floor((count + (group - 1)) * (1.0 / group))
    wide = jnp.broadcast_to(groups, (n_keys, 128)).astype(BF16)
    lower = (iota((n_keys, n_keys), 1) < iota((n_keys, n_keys), 0)).astype(F32).astype(BF16)
    base = mm(lower, wide)[:, :1] * group
    pos = jnp.sum(hot_f * (rank + base), axis=0, keepdims=True)
    opens = jnp.sum(hot_f * rank, axis=0, keepdims=True) < 0.5
    place = (iota((SLOTS, cap), 0) == pos.astype(I32)).astype(F32).astype(BF16)
    which = iota((8, cap), 0)
    slot = iota((8, cap), 1)
    vals = jnp.where(
        which == 0,
        slot >> 4,
        jnp.where(
            which == 1,
            slot & 15,
            jnp.where(which == 2, cols, jnp.where(which == 3, rows, jnp.where(which == 4, 1, opens.astype(I32)))),
        ),
    )
    vals = vals.astype(F32).astype(BF16)
    found = lax.dot_general(vals, place, (((1,), (1,)), ((), ())), preferred_element_type=F32)
    f = found.astype(I32)
    code = ((f[0:1] * 16 + f[1:2]) << CODE_BITS) | (f[2:3] << ROW_BITS) | f[3:4]
    code = jnp.where(f[4:5] > 0, code, cap << CODE_BITS)
    code = code | (f[5:6] << FRESH)
    last = jnp.where(groups > 0.5, base * (1.0 / group) + groups - 1.0, 1.0 * EMPTY)
    square = (n_keys, SLOTS)
    last = jnp.sum(jnp.where(iota(square, 0) == iota(square, 1), last, 0.0), axis=0, keepdims=True)
    return jnp.where(iota((8, SLOTS), 0) == 0, code, last.astype(I32))


def gather_kernel(
    feat, deg, rows, cols, out, fwd_list, bwd_list, mine, s1, r1, s2, r2, own_sem
):
    place = Place("row")
    lane = iota((128, 128), 1)
    perm = (iota((128, 128), 0) == ((lane & 15) * 8 + (lane >> 4))).astype(F32).astype(BF16)
    degrees = mm(deg[...].astype(F32).astype(BF16), perm)
    bucket = iota((1, 128), 1) >> 4
    shrink = jnp.zeros((1, 128), F32)
    for b in range(8):
        shrink = jnp.where(bucket == b, 2.0**-b, shrink)
    inverse = lax.rsqrt(degrees)
    for t in range(4):
        turned = lax.dot_general(
            feat[t * 128 : (t + 1) * 128, :], perm, (((0,), (0,)), ((), ())), preferred_element_type=F32
        )
        mine[t] = (turned * inverse[t : t + 1, :] * shrink).astype(BF16)
    barrier = pltpu.get_barrier_semaphore()
    partners = ["x", "om", "op", "twin"]
    for name in partners:
        pl.semaphore_signal(barrier, inc=1, device_id=place.device(name), device_id_type=MESH)
    pl.semaphore_wait(barrier, len(partners))
    sent = []
    chunks = [spread(place, mine, out, (s1, r1), (s2, r2), c, sent) for c in range(2)]
    for chunk in chunks:
        next(chunk)
    own = pltpu.make_async_copy(mine, out.at[pl.ds(place.index("o") * 4, 4)], own_sem)
    own.start()
    r, c = rows[...], cols[...]
    fwd_list[...] = order_list(r, r, c, 1 << ROW_BITS, GROUP)
    bwd_list[...] = order_list(c, r, c, 1 << COL_BITS, GROUP)
    own.wait()
    together(*chunks)
    for copy in sent:
        copy.wait_send()


def unpack(held, codes):
    words = jnp.concatenate([held[pl.ds((k >> CODE_BITS) & 1023, 1)] for k in codes], axis=0)
    parts = [(words & (1 << b)).astype(F32).astype(BF16) for b in range(8)]
    return jnp.concatenate(parts, axis=1)


def run_tiles(rounds, codes, product, acc, run):
    acc[...] = jnp.zeros_like(acc)

    def body(i, carry):
        total = acc[...]
        for u in range(UNROLL):
            at = (i * UNROLL + u) * GROUP
            code = [codes[0, at + g] for g in range(GROUP)]
            keep = (1 - ((code[0] >> FRESH) & 1)).astype(F32)
            total = total * keep + product(code)
            run[i * UNROLL + u] = total
        acc[...] = total
        return carry

    lax.fori_loop(0, rounds, body, 0)


def main_kernel(
    scale, n_row, n_col, fwd, bwd, src, masks, weight, deg_t, deg_s, cot, act, out, gw_out,
    held, acc, run, targets, mine, staged_c, got_c, twin_out, from_twin, staged_r, got_r,
    gw, gw_got, gw_row, gw_col, gw_all,
    sc, rc, sg, rg, s0, r0, sr, rr, s2, r2, s3, r3, s4, r4, mask_sem, own_sem,
):
    row = lax.axis_index("row")
    col = lax.axis_index("col")
    rows_place, cols_place = Place("row"), Place("col")
    load = pltpu.make_async_copy(masks, held.at[pl.ds(0, 768)], mask_sem)
    load.start()
    barrier = pltpu.get_barrier_semaphore()

    def row_peer(step):
        return {"row": lax.rem(row + step, n_row)}

    def col_peer(step):
        return {"col": lax.rem(col + step, n_col)}

    for step in range(1, n_row):
        pl.semaphore_signal(barrier, inc=1, device_id=row_peer(step), device_id_type=MESH)
    for step in range(1, n_col):
        pl.semaphore_signal(barrier, inc=1, device_id=col_peer(step), device_id_type=MESH)
    held[768] = jnp.zeros((16, 128), I32)
    run[EMPTY] = jnp.zeros((128, 128), F32)
    load.wait()

    def forward(code):
        lhs = jnp.concatenate(
            [src[(k >> ROW_BITS) & ((1 << COL_BITS) - 1)] for k in code], axis=1
        )
        return mm(lhs, unpack(held, code).reshape(GROUP * 128, 128))

    run_tiles(FWD_ROUNDS, fwd, forward, acc, run)
    pl.semaphore_wait(barrier, n_row + n_col - 2)
    sent = []

    def forward_sum(name, t):
        return run[fwd[1, cols_place.index(name) * 4 + t]]

    ups = [
        gather_up(cols_place, lambda name: None, forward_sum, staged_c, got_c, (sc, rc), c, sent)
        for c in range(2)
    ]
    for _ in range(5):
        for up in ups:
            next(up)
    w = weight[...]
    inverse = lax.rsqrt(deg_t[...].astype(F32))
    total = jnp.zeros((128, 256), F32)
    downs = []
    for c in range(2):
        next(ups[c])
        for t in (2 * c, 2 * c + 1):
            summed = gathered_tile(forward_sum, got_c, t)
            factor = jnp.broadcast_to(inverse[t : t + 1, :], (128, 128))
            agg_t = summed * factor
            factor = factor.T
            factor = jnp.concatenate([factor, factor], axis=1)
            t_hi, t_lo = split(agg_t)
            hi, lo = split(agg_t.T)
            pre = mm(hi, w) + mm(lo, w)
            slope = jnp.where(pre > 0, 1.0, jnp.exp(jnp.minimum(pre, 0.0)))
            rows = pl.ds(t * 128, 128)
            act[rows, :] = jnp.where(pre > 0, pre, slope - 1.0).astype(BF16)
            grad = cot[rows, :].astype(F32) * slope
            g_hi, g_lo = split(grad)
            total = total + (mm(t_hi, g_hi) + (mm(t_lo, g_hi) + mm(t_hi, g_lo)))
            scaled = (grad * factor).astype(BF16)
            mine[t] = lax.dot_general(
                scaled, w, (((1,), (1,)), ((), ())), preferred_element_type=F32
            ).astype(BF16)
        down = spread(cols_place, mine, targets, (sg, rg), None, c, sent)
        next(down)
        downs.append(down)
    own = pltpu.make_async_copy(mine, targets.at[pl.ds(col * 4, 4)], own_sem)
    own.start()
    gw[...] = total * scale
    weights = [
        send(
            gw.at[pl.ds(lax.rem(row + step, n_row) * 8, 8)],
            gw_got.at[step],
            (s2, r2),
            step,
            row_peer(step),
        )
        for step in range(1, n_row)
    ]
    own.wait()
    together(*downs)

    def backward(code):
        rhs = jnp.concatenate([targets[k & ((1 << ROW_BITS) - 1)] for k in code], axis=0)
        tiles = unpack(held, code)
        return mm(jnp.concatenate([tiles[g] for g in range(GROUP)], axis=1), rhs)

    run_tiles(BWD_ROUNDS, bwd, backward, acc, run)

    order = ["x2", "xm", "xp", "o2", "x", "om", "op", "o"]
    for k, name in enumerate(order):
        index = rows_place.chip(name) * 2 + 1 - rows_place.core
        for t in range(4):
            twin_out[k, t] = run[bwd[1, index * 4 + t]].astype(BF16)
        sent.append(
            send(twin_out.at[k], from_twin.at[k], (s0, r0), k, rows_place.device("twin"))
        )
    for copy in weights:
        copy.wait()
    summed = gw[pl.ds(row * 8, 8), :]
    for step in range(1, n_row):
        summed = summed + gw_got[step]
    gw_row[...] = summed
    gw_col[pl.ds(col, 1)] = summed[None]
    for step in range(1, n_col):
        sent.append(send(gw_row, gw_col.at[col], (s3, r3), step, col_peer(step)))

    arrived = set()

    def ready(name):
        if name not in arrived:
            k = order.index(name)
            landed(from_twin.at[k], r0.at[k])
            arrived.add(name)

    def backward_sum(name, t):
        mine_sum = run[bwd[1, rows_place.index(name) * 4 + t]]
        return mine_sum + from_twin[order.index(name), t].astype(F32)

    ups = [
        gather_up(rows_place, ready, backward_sum, staged_r, got_r, (sr, rr), c, sent)
        for c in range(2)
    ]
    for _ in range(4):
        for up in ups:
            next(up)
    for step in range(1, n_col):
        landed(gw_col.at[lax.rem(col + n_col - step, n_col)], r3.at[step])
    summed = gw_col[0]
    for c in range(1, n_col):
        summed = summed + gw_col[c]
    gw_mine = gw_all.at[pl.ds(row * 8, 8)]
    gw_all[pl.ds(row * 8, 8), :] = summed
    weights = [send(gw_mine, gw_mine, (s4, r4), step, row_peer(step)) for step in range(1, n_row)]
    inverse = lax.rsqrt(deg_s[...].astype(F32))
    for up in ups:
        next(up)
    bucket = iota((128, 128), 0) >> 4
    grow = jnp.zeros((128, 128), F32)
    for b in range(8):
        grow = jnp.where(bucket == b, 2.0**-b, grow)
    for c in range(2):
        next(ups[c])
        for t in (2 * c, 2 * c + 1):
            factor = jnp.broadcast_to(inverse[t : t + 1, :], (128, 128)).T
            summed = gathered_tile(backward_sum, got_r, t) * grow
            for b in range(8):
                out[pl.ds(t * 128 + b, 16, stride=8), :] = summed[b * 16 : (b + 1) * 16, :]
            rows = pl.ds(t * 128, 128)
            out[rows, :] = out[rows, :] * factor
    for copy in sent:
        copy.wait_send()
    for copy in weights:
        copy.wait_send()
    for step in range(1, n_row):
        peer = lax.rem(row + n_row - step, n_row)
        landed(gw_all.at[pl.ds(peer * 8, 8)], r4.at[step])
    gw_out[...] = gw_all[...]


def spec(space=VMEM):
    return pl.BlockSpec(memory_space=space)


def shaped(shape, dtype):
    return jax.ShapeDtypeStruct(shape, dtype)


def remote_params(number):
    return pltpu.CompilerParams(
        collective_id=number, has_side_effects=True, vmem_limit_bytes=BIG
    )


def dma(count):
    return pltpu.SemaphoreType.DMA((count,))


def body(features, weight, degrees, tile_rows, tile_cols, tile_masks, cotangent):
    row = lax.axis_index("row")
    col = lax.axis_index("col")
    n_row = lax.axis_size("row")
    n_col = lax.axis_size("col")
    deg = degrees.reshape(n_row * n_col, 4, 128)
    deg_s = lax.dynamic_index_in_dim(deg, col * n_row + row, 0, False)
    deg_t = lax.dynamic_index_in_dim(deg, row * n_col + col, 0, False)
    rows = tile_rows.reshape(1, -1)
    cols = tile_cols.reshape(1, -1)
    masks = tile_masks.reshape(-1, 16, 128)
    hbm = spec(pl.ANY)
    n_rt, n_ct = 4 * n_col, 4 * n_row

    gathered, fwd_list, bwd_list = pl.pallas_call(
        gather_kernel,
        out_shape=(
            shaped((n_ct, 128, 128), BF16),
            shaped((8, SLOTS), I32),
            shaped((8, SLOTS), I32),
        ),
        in_specs=[spec()] * 4,
        out_specs=(hbm, spec(), spec()),
        scratch_shapes=[
            VMEM((4, 128, 128), BF16),
            dma(20),
            dma(20),
            dma(20),
            dma(20),
            pltpu.SemaphoreType.DMA,
        ],
        compiler_params=remote_params(0),
        name="gather_sources",
    )(features, deg_s, rows, cols)

    smem = spec(pltpu.SMEM)
    block = (4, 128, 128)
    return pl.pallas_call(
        functools.partial(main_kernel, (512 * n_row * n_col) ** -0.5, n_row, n_col),
        out_shape=(
            shaped((512, 256), BF16),
            shaped((512, 128), F32),
            shaped((128, 256), F32),
        ),
        in_specs=[smem, smem, spec(), hbm, spec(), spec(), spec(), spec()],
        out_specs=(spec(), spec(), spec()),
        scratch_shapes=[
            VMEM((776, 16, 128), I32),
            VMEM((128, 128), F32),
            VMEM((EMPTY + 8, 128, 128), F32),
            VMEM((n_rt, 128, 128), BF16),
            VMEM(block, BF16),
            VMEM((7,) + block, BF16),
            VMEM((7,) + block, BF16),
            VMEM((8,) + block, BF16),
            VMEM((8,) + block, BF16),
            VMEM((7,) + block, BF16),
            VMEM((7,) + block, BF16),
            VMEM((128, 256), F32),
            VMEM((n_row, 8, 256), F32),
            VMEM((8, 256), F32),
            VMEM((n_col, 8, 256), F32),
            VMEM((128, 256), F32),
            dma(16),
            dma(16),
            dma(20),
            dma(20),
            dma(8),
            dma(8),
            dma(16),
            dma(16),
            dma(n_row),
            dma(n_row),
            dma(n_col),
            dma(n_col),
            dma(n_row),
            dma(n_row),
            pltpu.SemaphoreType.DMA,
            pltpu.SemaphoreType.DMA,
        ],
        compiler_params=remote_params(1),
        name="layer",
    )(fwd_list, bwd_list, gathered, masks, weight, deg_t, deg_s, cotangent)


def solution(mesh):
    in_specs = (
        P(("col", "row"), None),
        P(),
        P(),
        P("row", "col", None),
        P("row", "col", None),
        P("row", "col", None, None, None),
        P(("row", "col"), None),
    )
    out_specs = (P(("row", "col"), None), P(("col", "row"), None), P())
    return jax.shard_map(body, mesh=mesh, in_specs=in_specs, out_specs=out_specs, check_vma=False)
```

```python
import functools

import jax
import jax.numpy as jnp
from jax import lax
from jax.experimental import pallas as pl
from jax.experimental.pallas import tpu as pltpu
from jax.sharding import PartitionSpec as P

F32 = jnp.float32
BF16 = jnp.bfloat16
I32 = jnp.int32
MESH = pl.DeviceIdType.MESH
VMEM = pltpu.VMEM
SLOTS = 1024
ROW_BITS = 5
COL_BITS = 6
CODE_BITS = ROW_BITS + COL_BITS
FRESH = 24
GROUP = 4
FWD_ROUNDS, FWD_UNROLL = 8, 27
BWD_ROUNDS, BWD_UNROLL = 8, 30
EMPTY = BWD_ROUNDS * BWD_UNROLL
BIG = 56 * 1024 * 1024


def mm(a, b):
    return jnp.dot(a, b, preferred_element_type=F32)


def iota(shape, dim):
    return lax.broadcasted_iota(I32, shape, dim)


def split(x):
    hi = x.astype(BF16)
    return hi, (x - hi.astype(F32)).astype(BF16)


class Place:
    def __init__(self, axis):
        self.axis = axis
        me = lax.axis_index(axis)
        if axis == "row":
            self.core = lax.rem(me, 2)
            chip = me // 2
        else:
            self.core = None
            chip = me
        self.p, self.q = chip // 4, lax.rem(chip, 4)

    def chip(self, name):
        p = 1 - self.p if name[0] == "x" else self.p
        turn = {"": 0, "m": 3, "p": 1, "2": 2}[name[1:]]
        return p * 4 + lax.rem(self.q + turn, 4)

    def index(self, name):
        chip = self.chip(name)
        return chip if self.core is None else chip * 2 + self.core

    def device(self, name):
        if name == "twin":
            return {self.axis: (self.p * 4 + self.q) * 2 + 1 - self.core}
        return {self.axis: self.index(name)}

    def partners(self):
        return ["x", "om", "op"] + ([] if self.core is None else ["twin"])


def send(src, dst, sems, i, device):
    copy = pltpu.make_async_remote_copy(
        src_ref=src,
        dst_ref=dst,
        send_sem=sems[0].at[i],
        recv_sem=sems[1].at[i],
        device_id=device,
        device_id_type=MESH,
    )
    copy.start()
    return copy


def landed(ref, sem):
    pltpu.make_async_copy(ref, ref, sem).wait()


class Place:
    def __init__(self, axis):
        self.axis = axis
        me = lax.axis_index(axis)
        if axis == "row":
            self.core = lax.rem(me, 2)
            chip = me // 2
        else:
            self.core = None
            chip = me
        self.p, self.q = chip // 4, lax.rem(chip, 4)

    def chip(self, name):
        p = 1 - self.p if name[0] == "x" else self.p
        turn = {"": 0, "m": 3, "p": 1, "2": 2}[name[1:]]
        return p * 4 + lax.rem(self.q + turn, 4)

    def index(self, name):
        chip = self.chip(name)
        return chip if self.core is None else chip * 2 + self.core

    def device(self, name):
        if name == "twin":
            return {self.axis: (self.p * 4 + self.q) * 2 + 1 - self.core}
        return {self.axis: self.index(name)}

def send(src, dst, sems, i, device):
    copy = pltpu.make_async_remote_copy(
        src_ref=src,
        dst_ref=dst,
        send_sem=sems[0].at[i],
        recv_sem=sems[1].at[i],
        device_id=device,
        device_id_type=MESH,
    )
    copy.start()
    return copy


def landed(ref, sem):
    pltpu.make_async_copy(ref, ref, sem).wait()


NAMES = ["x", "om", "op", "o2", "xm", "xp", "x2"]


ROUTES = (("x", "op"), ("x", "om"))
SOURCE = {"x": "o2", "op": "xm", "om": "xp"}


def together(*parts):
    for steps in zip(*parts):
        pass


def spread_start(place, mine, out, sems, twin_sems, chunk, sent):
    own = mine.at[pl.ds(2 * chunk, 2)]
    here = out.at[pl.ds(place.index("o") * 4 + 2 * chunk, 2)]
    for i, to in enumerate(("x", "op", "om")):
        sent.append(send(own, here, sems, 8 * chunk + i, place.device(to)))
    if place.core is not None:
        sent.append(send(own, here, twin_sems, 8 * chunk + 7, place.device("twin")))


def spread(place, out, sems, twin_sems, chunk, sent):
    low = 8 * chunk

    def part(index, first=0, tiles=2):
        return out.at[pl.ds(index * 4 + 2 * chunk + first, tiles)]

    def wait(i, name, first=0, tiles=2):
        landed(part(place.index(name), first, tiles), sems[1].at[low + i])

    def pass_on(i, to, name, first=0, tiles=2):
        ref = part(place.index(name), first, tiles)
        sent.append(send(ref, ref, sems, low + i, place.device(to)))

    def twin(*names):
        if place.core is not None:
            for name in names:
                ref = part(place.index(name))
                i = low + NAMES.index(name)
                sent.append(send(ref, ref, twin_sems, i, place.device("twin")))

    wait(0, "x")
    pass_on(3, "op", "x")
    wait(2, "op")
    pass_on(4, "x", "op")
    pass_on(5, "om", "op")
    wait(1, "om")
    twin("x", "op", "om")
    yield
    wait(3, "xm")
    wait(4, "xp")
    wait(5, "o2")
    for t, to in enumerate(ROUTES[chunk]):
        pass_on(6 + t, to, SOURCE[to], t, 1)
    twin("xm", "xp", "o2")
    yield
    for t in range(2):
        wait(6 + t, "x2", t, 1)
    twin("x2")
    yield
    if place.core is not None:
        for i, name in enumerate(NAMES + ["o"]):
            index = place.chip(name) * 2 + 1 - place.core
            landed(part(index), twin_sems[1].at[low + i])
    yield


def gather_up(place, ready, value, staged, got, sems, chunk, sent):
    low = 8 * chunk
    both = (2 * chunk, 2 * chunk + 1)

    def go(i, slot, into, to, tiles=both):
        at = pl.ds(tiles[0], len(tiles))
        sent.append(send(staged.at[slot, at], got.at[into, at], sems, low + i, place.device(to)))

    def wait(i, into, tiles=both):
        landed(got.at[into, pl.ds(tiles[0], len(tiles))], sems[1].at[low + i])

    def stage(name, slot, *added):
        ready(name)
        for t in both:
            total = value(name, t)
            for into, tiles in added:
                if t in tiles:
                    total = total + got[into, t].astype(F32)
            staged[slot, t] = total.astype(BF16)

    stage("x2", 0)
    go(0, 0, 0, "x", both[:1])
    go(1, 0, 0, ("om", "op")[chunk], both[1:])
    stage("om", 6)
    go(2, 6, 5, "om")
    yield
    if chunk == 0:
        stage("xp", 1)
        go(3, 1, 1, "x")
        wait(1, 0, both[1:])
        stage("xm", 2, (0, both[1:]))
        go(4, 2, 2, "om")
    else:
        stage("xm", 2)
        go(4, 2, 2, "om")
        wait(1, 0, both[1:])
        stage("xp", 1, (0, both[1:]))
        go(3, 1, 1, "x")
    wait(0, 0, both[:1])
    stage("o2", 3, (0, both[:1]))
    go(5, 3, 3, "op")
    yield
    wait(4, 2)
    stage("x", 4, (2, both))
    go(6, 4, 4, "x")
    wait(3, 1)
    wait(5, 3)
    stage("op", 5, (1, both), (3, both))
    go(7, 5, 6, "op")
    yield
    ready("o")
    for i, into in ((2, 5), (6, 4), (7, 6)):
        wait(i, into)
    yield


def gathered_tile(value, got, t):
    total = value("o", t)
    for i in (4, 5, 6):
        total = total + got[i, t].astype(F32)
    return total


def order_list(keys, rows, cols, n_keys, group):
    cap = keys.shape[1]
    hot = iota((n_keys, cap), 0) == keys
    hot_f = hot.astype(F32)
    upper = (iota((cap, cap), 0) < iota((cap, cap), 1)).astype(F32).astype(BF16)
    rank = mm(hot_f.astype(BF16), upper)
    count = jnp.sum(hot_f, axis=1, keepdims=True)
    groups = jnp.floor((count + (group - 1)) * (1.0 / group))
    wide = jnp.broadcast_to(groups, (n_keys, 128)).astype(BF16)
    lower = (iota((n_keys, n_keys), 1) < iota((n_keys, n_keys), 0)).astype(F32).astype(BF16)
    base = mm(lower, wide)[:, :1] * group
    pos = jnp.sum(hot_f * (rank + base), axis=0, keepdims=True)
    opens = jnp.sum(hot_f * rank, axis=0, keepdims=True) < 0.5
    place = (iota((SLOTS, cap), 0) == pos.astype(I32)).astype(F32).astype(BF16)
    which = iota((8, cap), 0)
    slot = iota((8, cap), 1)
    vals = jnp.where(
        which == 0,
        slot >> 4,
        jnp.where(
            which == 1,
            slot & 15,
            jnp.where(which == 2, cols, jnp.where(which == 3, rows, jnp.where(which == 4, 1, opens.astype(I32)))),
        ),
    )
    vals = vals.astype(F32).astype(BF16)
    found = lax.dot_general(vals, place, (((1,), (1,)), ((), ())), preferred_element_type=F32)
    f = found.astype(I32)
    code = ((f[0:1] * 16 + f[1:2]) << CODE_BITS) | (f[2:3] << ROW_BITS) | f[3:4]
    code = jnp.where(f[4:5] > 0, code, cap << CODE_BITS)
    code = code | (f[5:6] << FRESH)
    last = jnp.where(groups > 0.5, base * (1.0 / group) + groups - 1.0, 1.0 * EMPTY)
    square = (n_keys, SLOTS)
    last = jnp.sum(jnp.where(iota(square, 0) == iota(square, 1), last, 0.0), axis=0, keepdims=True)
    return jnp.where(iota((8, SLOTS), 0) == 0, code, last.astype(I32))


def gather_kernel(
    feat, degrees_all, rows, cols, out, fwd_list, bwd_list, mine, deg, s1, r1, s2, r2, own_sem, deg_sem
):
    place = Place("row")
    chip_block = lax.axis_index("col") * lax.axis_size("row") + lax.axis_index("row")
    load = pltpu.make_async_copy(degrees_all.at[chip_block], deg, deg_sem)
    load.start()
    barrier = pltpu.get_barrier_semaphore()
    partners = ["x", "om", "op", "twin"]
    for name in partners:
        pl.semaphore_signal(barrier, inc=1, device_id=place.device(name), device_id_type=MESH)
    lane = iota((128, 128), 1)
    perm = (iota((128, 128), 0) == ((lane & 15) * 8 + (lane >> 4))).astype(F32).astype(BF16)
    load.wait()
    degrees = mm(deg[...].astype(F32).astype(BF16), perm)
    bucket = iota((1, 128), 1) >> 4
    shrink = jnp.zeros((1, 128), F32)
    for b in range(8):
        shrink = jnp.where(bucket == b, 2.0**-b, shrink)
    inverse = lax.rsqrt(degrees)
    for t in range(4):
        turned = lax.dot_general(
            feat[t * 128 : (t + 1) * 128, :], perm, (((0,), (0,)), ((), ())), preferred_element_type=F32
        )
        mine[t] = (turned * inverse[t : t + 1, :] * shrink).astype(BF16)
    pl.semaphore_wait(barrier, len(partners))
    sent = []
    for c in range(2):
        spread_start(place, mine, out, (s1, r1), (s2, r2), c, sent)
    own = pltpu.make_async_copy(mine, out.at[pl.ds(place.index("o") * 4, 4)], own_sem)
    own.start()
    r, c = rows[...], cols[...]
    fwd_list[...] = order_list(r, r, c, 1 << ROW_BITS, GROUP)
    bwd_list[...] = order_list(c, r, c, 1 << COL_BITS, GROUP)
    own.wait()
    together(*[spread(place, out, (s1, r1), (s2, r2), c, sent) for c in range(2)])
    for copy in sent:
        copy.wait_send()


def unpack(held, codes):
    words = jnp.concatenate([held[pl.ds((k >> CODE_BITS) & 1023, 1)] for k in codes], axis=0)
    parts = [(words & (1 << b)).astype(F32).astype(BF16) for b in range(8)]
    return jnp.concatenate(parts, axis=1)


def run_tiles(start, stop, unroll, codes, product, acc, run):
    def body(i, carry):
        total = acc[...]
        for u in range(unroll):
            at = (i * unroll + u) * GROUP
            code = [codes[0, at + g] for g in range(GROUP)]
            keep = (1 - ((code[0] >> FRESH) & 1)).astype(F32)
            total = total * keep + product(code)
            run[i * unroll + u] = total
        acc[...] = total
        return carry

    lax.fori_loop(start, stop, body, 0)


def main_kernel(
    scale, n_row, n_col, fwd, bwd, src, masks, weight, degrees_all, cot, act, out, gw_out,
    deg_t, deg_s, held, acc, run, targets, mine, staged_c, got_c, twin_out, from_twin, staged_r, got_r,
    gw, gw_got, gw_row, gw_col, gw_all,
    sc, rc, sg, rg, s0, r0, sr, rr, s2, r2, s3, r3, s4, r4, mask_sem, own_sem, deg_sem,
):
    row = lax.axis_index("row")
    col = lax.axis_index("col")
    rows_place, cols_place = Place("row"), Place("col")
    load = pltpu.make_async_copy(masks, held.at[pl.ds(0, 768)], mask_sem)
    load.start()
    loads = [
        pltpu.make_async_copy(degrees_all.at[row * n_col + col], deg_t, deg_sem.at[0]),
        pltpu.make_async_copy(degrees_all.at[col * n_row + row], deg_s, deg_sem.at[1]),
    ]
    for copy in loads:
        copy.start()
    barrier = pltpu.get_barrier_semaphore()

    def row_peer(step):
        return {"row": lax.rem(row + step, n_row)}

    def col_peer(step):
        return {"col": lax.rem(col + step, n_col)}

    for step in range(1, n_row):
        pl.semaphore_signal(barrier, inc=1, device_id=row_peer(step), device_id_type=MESH)
    for step in range(1, n_col):
        pl.semaphore_signal(barrier, inc=1, device_id=col_peer(step), device_id_type=MESH)
    held[768] = jnp.zeros((16, 128), I32)
    run[EMPTY] = jnp.zeros((128, 128), F32)
    load.wait()
    for copy in loads:
        copy.wait()

    def forward(code):
        lhs = jnp.concatenate(
            [src[(k >> ROW_BITS) & ((1 << COL_BITS) - 1)] for k in code], axis=1
        )
        return mm(lhs, unpack(held, code).reshape(GROUP * 128, 128))

    acc[...] = jnp.zeros_like(acc)
    run_tiles(0, FWD_ROUNDS, FWD_UNROLL, fwd, forward, acc, run)
    pl.semaphore_wait(barrier, n_row + n_col - 2)
    sent = []

    def forward_sum(name, t):
        return run[fwd[1, cols_place.index(name) * 4 + t]]

    ups = [
        gather_up(cols_place, lambda name: None, forward_sum, staged_c, got_c, (sc, rc), c, sent)
        for c in range(2)
    ]
    for _ in range(3):
        for up in ups:
            next(up)
    w = weight[...]
    inverse = lax.rsqrt(deg_t[...].astype(F32))
    total = jnp.zeros((128, 256), F32)
    for c in range(2):
        next(ups[c])
        for t in (2 * c, 2 * c + 1):
            summed = gathered_tile(forward_sum, got_c, t)
            factor = jnp.broadcast_to(inverse[t : t + 1, :], (128, 128))
            agg_t = summed * factor
            factor = factor.T
            factor = jnp.concatenate([factor, factor], axis=1)
            t_hi, t_lo = split(agg_t)
            hi, lo = split(agg_t.T)
            pre = mm(hi, w) + mm(lo, w)
            slope = jnp.where(pre > 0, 1.0, jnp.exp(jnp.minimum(pre, 0.0)))
            rows = pl.ds(t * 128, 128)
            act[rows, :] = jnp.where(pre > 0, pre, slope - 1.0).astype(BF16)
            grad = cot[rows, :].astype(F32) * slope
            g_hi, g_lo = split(grad)
            total = total + (mm(t_hi, g_hi) + (mm(t_lo, g_hi) + mm(t_hi, g_lo)))
            scaled = (grad * factor).astype(BF16)
            mine[t] = lax.dot_general(
                scaled, w, (((1,), (1,)), ((), ())), preferred_element_type=F32
            ).astype(BF16)
        spread_start(cols_place, mine, targets, (sg, rg), None, c, sent)
    own = pltpu.make_async_copy(mine, targets.at[pl.ds(col * 4, 4)], own_sem)
    own.start()
    gw[...] = total * scale
    own.wait()
    together(*[spread(cols_place, targets, (sg, rg), None, c, sent) for c in range(2)])
    weights = [
        send(
            gw.at[pl.ds(lax.rem(row + step, n_row) * 8, 8)],
            gw_got.at[step],
            (s2, r2),
            step,
            row_peer(step),
        )
        for step in range(1, n_row)
    ]

    def backward(code):
        rhs = jnp.concatenate([targets[k & ((1 << ROW_BITS) - 1)] for k in code], axis=0)
        tiles = unpack(held, code)
        return mm(jnp.concatenate([tiles[g] for g in range(GROUP)], axis=1), rhs)

    acc[...] = jnp.zeros_like(acc)
    run_tiles(0, BWD_ROUNDS // 2, BWD_UNROLL, bwd, backward, acc, run)
    for copy in weights:
        copy.wait()
    summed = gw[pl.ds(row * 8, 8), :]
    for step in range(1, n_row):
        summed = summed + gw_got[step]
    gw_row[...] = summed
    gw_col[pl.ds(col, 1)] = summed[None]
    for step in range(1, n_col):
        sent.append(send(gw_row, gw_col.at[col], (s3, r3), step, col_peer(step)))
    run_tiles(BWD_ROUNDS // 2, BWD_ROUNDS, BWD_UNROLL, bwd, backward, acc, run)

    order = ["x2", "om", "xp", "xm", "o2", "x", "op", "o"]
    for k, name in enumerate(order):
        index = rows_place.chip(name) * 2 + 1 - rows_place.core
        for t in range(4):
            twin_out[k, t] = run[bwd[1, index * 4 + t]].astype(BF16)
        sent.append(
            send(twin_out.at[k], from_twin.at[k], (s0, r0), k, rows_place.device("twin"))
        )
    arrived = set()

    def ready(name):
        if name not in arrived:
            k = order.index(name)
            landed(from_twin.at[k], r0.at[k])
            arrived.add(name)

    def backward_sum(name, t):
        mine_sum = run[bwd[1, rows_place.index(name) * 4 + t]]
        return mine_sum + from_twin[order.index(name), t].astype(F32)

    ups = [
        gather_up(rows_place, ready, backward_sum, staged_r, got_r, (sr, rr), c, sent)
        for c in range(2)
    ]
    for up in ups:
        next(up)
    for step in range(1, n_col):
        landed(gw_col.at[lax.rem(col + n_col - step, n_col)], r3.at[step])
    summed = gw_col[0]
    for c in range(1, n_col):
        summed = summed + gw_col[c]
    gw_mine = gw_all.at[pl.ds(row * 8, 8)]
    gw_all[pl.ds(row * 8, 8), :] = summed
    weights = [send(gw_mine, gw_mine, (s4, r4), step, row_peer(step)) for step in range(1, n_row)]
    inverse = lax.rsqrt(deg_s[...].astype(F32))
    for _ in range(2):
        for up in ups:
            next(up)
    bucket = iota((128, 128), 0) >> 4
    grow = jnp.zeros((128, 128), F32)
    for b in range(8):
        grow = jnp.where(bucket == b, 2.0**-b, grow)
    for t in range(4):
        if t % 2 == 0:
            next(ups[t // 2])
        factor = jnp.broadcast_to(inverse[t : t + 1, :], (128, 128)).T
        summed = gathered_tile(backward_sum, got_r, t) * grow
        for b in range(8):
            out[pl.ds(t * 128 + b, 16, stride=8), :] = summed[b * 16 : (b + 1) * 16, :]
        rows = pl.ds(t * 128, 128)
        out[rows, :] = out[rows, :] * factor
    for copy in sent:
        copy.wait_send()
    for copy in weights:
        copy.wait_send()
    for step in range(1, n_row):
        peer = lax.rem(row + n_row - step, n_row)
        landed(gw_all.at[pl.ds(peer * 8, 8)], r4.at[step])
    gw_out[...] = gw_all[...]


def hand_on_kernel(a, b, c, a_out, b_out, c_out):
    a_out[...] = a[...]
    b_out[...] = b[...]
    c_out[...] = c[...]


def spec(space=VMEM):
    return pl.BlockSpec(memory_space=space)


def shaped(shape, dtype):
    return jax.ShapeDtypeStruct(shape, dtype)


def remote_params(number):
    return pltpu.CompilerParams(
        collective_id=number, has_side_effects=True, vmem_limit_bytes=BIG
    )


def dma(count):
    return pltpu.SemaphoreType.DMA((count,))


def body(features, weight, degrees, tile_rows, tile_cols, tile_masks, cotangent):
    n_row = lax.axis_size("row")
    n_col = lax.axis_size("col")
    deg = degrees.reshape(n_row * n_col, 4, 128)
    rows = tile_rows.reshape(1, -1)
    cols = tile_cols.reshape(1, -1)
    masks = tile_masks.reshape(-1, 16, 128)
    hbm = spec(pl.ANY)
    n_rt, n_ct = 4 * n_col, 4 * n_row

    gathered, fwd_list, bwd_list = pl.pallas_call(
        gather_kernel,
        out_shape=(
            shaped((n_ct, 128, 128), BF16),
            shaped((8, SLOTS), I32),
            shaped((8, SLOTS), I32),
        ),
        in_specs=[spec(), hbm, spec(), spec()],
        out_specs=(hbm, spec(), spec()),
        scratch_shapes=[
            VMEM((4, 128, 128), BF16),
            VMEM((4, 128), I32),
            dma(16),
            dma(16),
            dma(16),
            dma(16),
            pltpu.SemaphoreType.DMA,
            pltpu.SemaphoreType.DMA,
        ],
        compiler_params=remote_params(0),
        name="gather_sources",
    )(features, deg, rows, cols)

    smem = spec(pltpu.SMEM)
    outs = (
        shaped((512, 256), BF16),
        shaped((512, 128), F32),
        shaped((128, 256), F32),
    )
    block = (4, 128, 128)
    results = pl.pallas_call(
        functools.partial(main_kernel, (512 * n_row * n_col) ** -0.5, n_row, n_col),
        out_shape=outs,
        in_specs=[smem, smem, spec(), hbm, spec(), hbm, spec()],
        out_specs=(spec(), spec(), spec()),
        scratch_shapes=[
            VMEM((4, 128), I32),
            VMEM((4, 128), I32),
            VMEM((776, 16, 128), I32),
            VMEM((128, 128), F32),
            VMEM((EMPTY + 8, 128, 128), F32),
            VMEM((n_rt, 128, 128), BF16),
            VMEM(block, BF16),
            VMEM((7,) + block, BF16),
            VMEM((7,) + block, BF16),
            VMEM((8,) + block, BF16),
            VMEM((8,) + block, BF16),
            VMEM((7,) + block, BF16),
            VMEM((7,) + block, BF16),
            VMEM((128, 256), F32),
            VMEM((n_row, 8, 256), F32),
            VMEM((8, 256), F32),
            VMEM((n_col, 8, 256), F32),
            VMEM((128, 256), F32),
            dma(16),
            dma(16),
            dma(16),
            dma(16),
            dma(8),
            dma(8),
            dma(16),
            dma(16),
            dma(n_row),
            dma(n_row),
            dma(n_col),
            dma(n_col),
            dma(n_row),
            dma(n_row),
            pltpu.SemaphoreType.DMA,
            pltpu.SemaphoreType.DMA,
            dma(2),
        ],
        compiler_params=remote_params(1),
        name="layer",
    )(fwd_list, bwd_list, gathered, masks, weight, deg, cotangent)
    return pl.pallas_call(
        hand_on_kernel,
        out_shape=outs,
        in_specs=[spec()] * 3,
        out_specs=(spec(), spec(), spec()),
        name="results",
    )(*results)


def solution(mesh):
    in_specs = (
        P(("col", "row"), None),
        P(),
        P(),
        P("row", "col", None),
        P("row", "col", None),
        P("row", "col", None, None, None),
        P(("row", "col"), None),
    )
    out_specs = (P(("row", "col"), None), P(("col", "row"), None), P())
    return jax.shard_map(body, mesh=mesh, in_specs=in_specs, out_specs=out_specs, check_vma=False)
```

```python
import functools

import jax
import jax.numpy as jnp
from jax import lax
from jax.experimental import pallas as pl
from jax.experimental.pallas import tpu as pltpu
from jax.sharding import PartitionSpec as P

F32 = jnp.float32
BF16 = jnp.bfloat16
I32 = jnp.int32
MESH = pl.DeviceIdType.MESH
VMEM = pltpu.VMEM
SLOTS = 1024
ROW_BITS = 5
COL_BITS = 6
CODE_BITS = ROW_BITS + COL_BITS
FRESH = 24
GROUP = 4
FWD_ROUNDS, FWD_UNROLL = 8, 27
BWD_ROUNDS, BWD_UNROLL = 8, 30
EMPTY = BWD_ROUNDS * BWD_UNROLL
BIG = 56 * 1024 * 1024


def mm(a, b):
    return jnp.dot(a, b, preferred_element_type=F32)


def iota(shape, dim):
    return lax.broadcasted_iota(I32, shape, dim)


def split(x):
    hi = x.astype(BF16)
    return hi, (x - hi.astype(F32)).astype(BF16)


class Place:
    def __init__(self, axis):
        self.axis = axis
        me = lax.axis_index(axis)
        if axis == "row":
            self.core = lax.rem(me, 2)
            chip = me // 2
        else:
            self.core = None
            chip = me
        self.p, self.q = chip // 4, lax.rem(chip, 4)

    def chip(self, name):
        p = 1 - self.p if name[0] == "x" else self.p
        turn = {"": 0, "m": 3, "p": 1, "2": 2}[name[1:]]
        return p * 4 + lax.rem(self.q + turn, 4)

    def index(self, name):
        chip = self.chip(name)
        return chip if self.core is None else chip * 2 + self.core

    def device(self, name):
        if name == "twin":
            return {self.axis: (self.p * 4 + self.q) * 2 + 1 - self.core}
        return {self.axis: self.index(name)}

    def partners(self):
        return ["x", "om", "op"] + ([] if self.core is None else ["twin"])


def send(src, dst, sems, i, device):
    copy = pltpu.make_async_remote_copy(
        src_ref=src,
        dst_ref=dst,
        send_sem=sems[0].at[i],
        recv_sem=sems[1].at[i],
        device_id=device,
        device_id_type=MESH,
    )
    copy.start()
    return copy


def landed(ref, sem):
    pltpu.make_async_copy(ref, ref, sem).wait()


class Place:
    def __init__(self, axis):
        self.axis = axis
        me = lax.axis_index(axis)
        if axis == "row":
            self.core = lax.rem(me, 2)
            chip = me // 2
        else:
            self.core = None
            chip = me
        self.p, self.q = chip // 4, lax.rem(chip, 4)

    def chip(self, name):
        p = 1 - self.p if name[0] == "x" else self.p
        turn = {"": 0, "m": 3, "p": 1, "2": 2}[name[1:]]
        return p * 4 + lax.rem(self.q + turn, 4)

    def index(self, name):
        chip = self.chip(name)
        return chip if self.core is None else chip * 2 + self.core

    def device(self, name):
        if name == "twin":
            return {self.axis: (self.p * 4 + self.q) * 2 + 1 - self.core}
        return {self.axis: self.index(name)}

def send(src, dst, sems, i, device):
    copy = pltpu.make_async_remote_copy(
        src_ref=src,
        dst_ref=dst,
        send_sem=sems[0].at[i],
        recv_sem=sems[1].at[i],
        device_id=device,
        device_id_type=MESH,
    )
    copy.start()
    return copy


def landed(ref, sem):
    pltpu.make_async_copy(ref, ref, sem).wait()


NAMES = ["x", "om", "op", "o2", "xm", "xp", "x2"]


ROUTES = (("x", "op"), ("x", "om"))
SOURCE = {"x": "o2", "op": "xm", "om": "xp"}


def together(*parts):
    for steps in zip(*parts):
        pass


def spread_start(place, mine, out, sems, twin_sems, chunk, sent):
    own = mine.at[pl.ds(2 * chunk, 2)]
    here = out.at[pl.ds(place.index("o") * 4 + 2 * chunk, 2)]
    for i, to in enumerate(("x", "op", "om")):
        sent.append(send(own, here, sems, 8 * chunk + i, place.device(to)))
    if place.core is not None:
        sent.append(send(own, here, twin_sems, 8 * chunk + 7, place.device("twin")))


def spread(place, out, sems, twin_sems, chunk, sent):
    low = 8 * chunk

    def part(index, first=0, tiles=2):
        return out.at[pl.ds(index * 4 + 2 * chunk + first, tiles)]

    def wait(i, name, first=0, tiles=2):
        landed(part(place.index(name), first, tiles), sems[1].at[low + i])

    def pass_on(i, to, name, first=0, tiles=2):
        ref = part(place.index(name), first, tiles)
        sent.append(send(ref, ref, sems, low + i, place.device(to)))

    def twin(*names):
        if place.core is not None:
            for name in names:
                ref = part(place.index(name))
                i = low + NAMES.index(name)
                sent.append(send(ref, ref, twin_sems, i, place.device("twin")))

    wait(0, "x")
    pass_on(3, "op", "x")
    wait(2, "op")
    pass_on(4, "x", "op")
    pass_on(5, "om", "op")
    wait(1, "om")
    twin("x", "op", "om")
    yield
    wait(3, "xm")
    wait(4, "xp")
    wait(5, "o2")
    for t, to in enumerate(ROUTES[chunk]):
        pass_on(6 + t, to, SOURCE[to], t, 1)
    twin("xm", "xp", "o2")
    yield
    for t in range(2):
        wait(6 + t, "x2", t, 1)
    twin("x2")
    yield
    if place.core is not None:
        for i, name in enumerate(NAMES + ["o"]):
            index = place.chip(name) * 2 + 1 - place.core
            landed(part(index), twin_sems[1].at[low + i])
    yield


def gather_up(place, ready, value, staged, got, sems, chunk, sent):
    low = 8 * chunk
    both = (2 * chunk, 2 * chunk + 1)

    def go(i, slot, into, to, tiles=both):
        at = pl.ds(tiles[0], len(tiles))
        sent.append(send(staged.at[slot, at], got.at[into, at], sems, low + i, place.device(to)))

    def wait(i, into, tiles=both):
        landed(got.at[into, pl.ds(tiles[0], len(tiles))], sems[1].at[low + i])

    def stage(name, slot, *added):
        ready(name)
        for t in both:
            total = value(name, t)
            for into, tiles in added:
                if t in tiles:
                    total = total + got[into, t].astype(F32)
            staged[slot, t] = total.astype(BF16)

    stage("x2", 0)
    go(0, 0, 0, "x", both[:1])
    go(1, 0, 0, ("om", "op")[chunk], both[1:])
    stage("om", 6)
    go(2, 6, 5, "om")
    yield
    if chunk == 0:
        stage("xp", 1)
        go(3, 1, 1, "x")
        wait(1, 0, both[1:])
        stage("xm", 2, (0, both[1:]))
        go(4, 2, 2, "om")
    else:
        stage("xm", 2)
        go(4, 2, 2, "om")
        wait(1, 0, both[1:])
        stage("xp", 1, (0, both[1:]))
        go(3, 1, 1, "x")
    wait(0, 0, both[:1])
    stage("o2", 3, (0, both[:1]))
    go(5, 3, 3, "op")
    yield
    wait(4, 2)
    stage("x", 4, (2, both))
    go(6, 4, 4, "x")
    wait(3, 1)
    wait(5, 3)
    stage("op", 5, (1, both), (3, both))
    go(7, 5, 6, "op")
    yield
    ready("o")
    for i, into in ((2, 5), (6, 4), (7, 6)):
        wait(i, into)
    yield


def gathered_tile(value, got, t):
    total = value("o", t)
    for i in (4, 5, 6):
        total = total + got[i, t].astype(F32)
    return total


def order_list(keys, rows, cols, n_keys, group):
    cap = keys.shape[1]
    hot = iota((n_keys, cap), 0) == keys
    hot_f = hot.astype(F32)
    upper = (iota((cap, cap), 0) < iota((cap, cap), 1)).astype(F32).astype(BF16)
    rank = mm(hot_f.astype(BF16), upper)
    count = jnp.sum(hot_f, axis=1, keepdims=True)
    groups = jnp.floor((count + (group - 1)) * (1.0 / group))
    wide = jnp.broadcast_to(groups, (n_keys, 128)).astype(BF16)
    lower = (iota((n_keys, n_keys), 1) < iota((n_keys, n_keys), 0)).astype(F32).astype(BF16)
    base = mm(lower, wide)[:, :1] * group
    pos = jnp.sum(hot_f * (rank + base), axis=0, keepdims=True)
    opens = jnp.sum(hot_f * rank, axis=0, keepdims=True) < 0.5
    place = (iota((SLOTS, cap), 0) == pos.astype(I32)).astype(F32).astype(BF16)
    which = iota((8, cap), 0)
    slot = iota((8, cap), 1)
    vals = jnp.where(
        which == 0,
        slot >> 4,
        jnp.where(
            which == 1,
            slot & 15,
            jnp.where(which == 2, cols, jnp.where(which == 3, rows, jnp.where(which == 4, 1, opens.astype(I32)))),
        ),
    )
    vals = vals.astype(F32).astype(BF16)
    found = lax.dot_general(vals, place, (((1,), (1,)), ((), ())), preferred_element_type=F32)
    f = found.astype(I32)
    code = ((f[0:1] * 16 + f[1:2]) << CODE_BITS) | (f[2:3] << ROW_BITS) | f[3:4]
    code = jnp.where(f[4:5] > 0, code, cap << CODE_BITS)
    code = code | (f[5:6] << FRESH)
    last = jnp.where(groups > 0.5, base * (1.0 / group) + groups - 1.0, 1.0 * EMPTY)
    square = (n_keys, SLOTS)
    last = jnp.sum(jnp.where(iota(square, 0) == iota(square, 1), last, 0.0), axis=0, keepdims=True)
    return jnp.where(iota((8, SLOTS), 0) == 0, code, last.astype(I32))


def scale_sources(feat, deg, mine):
    lane = iota((128, 128), 1)
    perm = (iota((128, 128), 0) == ((lane & 15) * 8 + (lane >> 4))).astype(F32).astype(BF16)
    degrees = mm(deg[...].astype(F32).astype(BF16), perm)
    bucket = iota((1, 128), 1) >> 4
    shrink = jnp.zeros((1, 128), F32)
    for b in range(8):
        shrink = jnp.where(bucket == b, 2.0**-b, shrink)
    inverse = lax.rsqrt(degrees)
    for t in range(4):
        turned = lax.dot_general(
            feat[t * 128 : (t + 1) * 128, :], perm, (((0,), (0,)), ((), ())), preferred_element_type=F32
        )
        factor = inverse[t : t + 1, :] * shrink
        mine[t] = (turned * factor).astype(BF16)
    return [inverse[t : t + 1, :] * shrink for t in range(4)]


def unpack(held, codes):
    words = jnp.concatenate([held[pl.ds(jnp.minimum((k >> CODE_BITS) & 1023, 768), 1)] for k in codes], axis=0)
    parts = [(words & (1 << b)).astype(F32).astype(BF16) for b in range(8)]
    return jnp.concatenate(parts, axis=1)


def entry(codes, key):
    return jnp.clip(codes[1, key], 0, EMPTY)


def run_tiles(start, stop, unroll, codes, product, acc, run):
    def body(i, carry):
        total = acc[...]
        for u in range(unroll):
            at = (i * unroll + u) * GROUP
            code = [codes[0, at + g] for g in range(GROUP)]
            keep = (1 - ((code[0] >> FRESH) & 1)).astype(F32)
            total = total * keep + product(code)
            run[i * unroll + u] = total
        acc[...] = total
        return carry

    lax.fori_loop(start, stop, body, 0)


def main_kernel(
    scale, n_row, n_col, rows, cols, feat, masks, weight, degrees_all, cot, act, out, gw_out,
    fwd, bwd, fwd_list, bwd_list, out_factor, back_factor, deg_t, deg_s, src, source, held, acc, run, targets, mine, staged_c, got_c, twin_out, from_twin, staged_r, got_r,
    agg_hold, grad_hold, gw, gw_got, gw_row, gw_col, gw_all,
    sa, ra, st, rt, sc, rc, sg, rg, s0, r0, sr, rr, s2, r2, s3, r3, s4, r4, mask_sem, own_sem, deg_sem, list_sem,
):
    row = lax.axis_index("row")
    col = lax.axis_index("col")
    rows_place, cols_place = Place("row"), Place("col")
    load = pltpu.make_async_copy(masks, held.at[pl.ds(0, 768)], mask_sem)
    load.start()
    loads = [
        pltpu.make_async_copy(degrees_all.at[row * n_col + col], deg_t, deg_sem.at[0]),
        pltpu.make_async_copy(degrees_all.at[col * n_row + row], deg_s, deg_sem.at[1]),
    ]
    for copy in loads:
        copy.start()
    barrier = pltpu.get_barrier_semaphore()

    def row_peer(step):
        return {"row": lax.rem(row + step, n_row)}

    def col_peer(step):
        return {"col": lax.rem(col + step, n_col)}

    for step in range(1, n_row):
        pl.semaphore_signal(barrier, inc=1, device_id=row_peer(step), device_id_type=MESH)
    for step in range(1, n_col):
        pl.semaphore_signal(barrier, inc=1, device_id=col_peer(step), device_id_type=MESH)
    held[768] = jnp.zeros((16, 128), I32)
    run[EMPTY] = jnp.zeros((128, 128), F32)
    for copy in loads:
        copy.wait()
    back_factors = scale_sources(feat, deg_s, source)
    own = pltpu.make_async_copy(source, src.at[pl.ds(rows_place.index("o") * 4, 4)], own_sem)
    own.start()
    pl.semaphore_wait(barrier, n_row + n_col - 2)
    sent = []
    for c in range(2):
        spread_start(rows_place, source, src, (sa, ra), (st, rt), c, sent)
    r, c = rows[...], cols[...]
    fwd_list[...] = order_list(r, r, c, 1 << ROW_BITS, GROUP)
    bwd_list[...] = order_list(c, r, c, 1 << COL_BITS, GROUP)
    lists = [
        pltpu.make_async_copy(fwd_list, fwd, list_sem.at[0]),
        pltpu.make_async_copy(bwd_list, bwd, list_sem.at[1]),
    ]
    for copy in lists:
        copy.start()
    inverse = lax.rsqrt(deg_t[...].astype(F32))
    for t in range(4):
        back_factor[t] = jnp.broadcast_to(back_factors[t], (128, 128)).T
        out_factor[t] = jnp.broadcast_to(inverse[t : t + 1, :], (128, 128)).T
    own.wait()
    together(*[spread(rows_place, src, (sa, ra), (st, rt), c, sent) for c in range(2)])
    load.wait()
    for copy in lists:
        copy.wait()

    def forward(code):
        lhs = jnp.concatenate(
            [src[(k >> ROW_BITS) & ((1 << COL_BITS) - 1)] for k in code], axis=1
        )
        return mm(lhs, unpack(held, code).reshape(GROUP * 128, 128))

    acc[...] = jnp.zeros_like(acc)
    run_tiles(0, FWD_ROUNDS, FWD_UNROLL, fwd, forward, acc, run)

    def forward_sum(name, t):
        return run[entry(fwd, cols_place.index(name) * 4 + t)]

    ups = [
        gather_up(cols_place, lambda name: None, forward_sum, staged_c, got_c, (sc, rc), c, sent)
        for c in range(2)
    ]
    for _ in range(3):
        for up in ups:
            next(up)
    w = weight[...]
    for c in range(2):
        next(ups[c])
        for t in (2 * c, 2 * c + 1):
            summed = gathered_tile(forward_sum, got_c, t)
            agg_t = summed * inverse[t : t + 1, :]
            factor = out_factor[t]
            factor = jnp.concatenate([factor, factor], axis=1)
            hi, lo = split(agg_t.T)
            pre = mm(hi, w) + mm(lo, w)
            slope = jnp.where(pre > 0, 1.0, jnp.exp(jnp.minimum(pre, 0.0)))
            here = pl.ds(t * 128, 128)
            act[here, :] = jnp.where(pre > 0, pre, slope - 1.0).astype(BF16)
            grad = cot[here, :].astype(F32) * slope
            agg_hold[t] = agg_t
            grad_hold[t] = grad
            scaled = (grad * factor).astype(BF16)
            mine[t] = lax.dot_general(
                scaled, w, (((1,), (1,)), ((), ())), preferred_element_type=F32
            ).astype(BF16)
        spread_start(cols_place, mine, targets, (sg, rg), None, c, sent)
    own = pltpu.make_async_copy(mine, targets.at[pl.ds(col * 4, 4)], own_sem)
    own.start()
    total = jnp.zeros((128, 256), F32)
    for t in range(4):
        t_hi, t_lo = split(agg_hold[t])
        g_hi, g_lo = split(grad_hold[t])
        total = total + (mm(t_hi, g_hi) + (mm(t_lo, g_hi) + mm(t_hi, g_lo)))
    gw[...] = total * scale
    own.wait()
    together(*[spread(cols_place, targets, (sg, rg), None, c, sent) for c in range(2)])
    weights = [
        send(
            gw.at[pl.ds(lax.rem(row + step, n_row) * 8, 8)],
            gw_got.at[step],
            (s2, r2),
            step,
            row_peer(step),
        )
        for step in range(1, n_row)
    ]

    def backward(code):
        rhs = jnp.concatenate([targets[k & ((1 << ROW_BITS) - 1)] for k in code], axis=0)
        tiles = unpack(held, code)
        return mm(jnp.concatenate([tiles[g] for g in range(GROUP)], axis=1), rhs)

    acc[...] = jnp.zeros_like(acc)
    run_tiles(0, BWD_ROUNDS // 2, BWD_UNROLL, bwd, backward, acc, run)
    for copy in weights:
        copy.wait()
    summed = gw[pl.ds(row * 8, 8), :]
    for step in range(1, n_row):
        summed = summed + gw_got[step]
    gw_row[...] = summed
    gw_col[pl.ds(col, 1)] = summed[None]
    for step in range(1, n_col):
        sent.append(send(gw_row, gw_col.at[col], (s3, r3), step, col_peer(step)))
    run_tiles(BWD_ROUNDS // 2, BWD_ROUNDS, BWD_UNROLL, bwd, backward, acc, run)

    order = ["x2", "om", "xp", "xm", "o2", "x", "op", "o"]
    for k, name in enumerate(order):
        index = rows_place.chip(name) * 2 + 1 - rows_place.core
        for t in range(4):
            twin_out[k, t] = run[entry(bwd, index * 4 + t)].astype(BF16)
        sent.append(
            send(twin_out.at[k], from_twin.at[k], (s0, r0), k, rows_place.device("twin"))
        )
    arrived = set()

    def ready(name):
        if name not in arrived:
            k = order.index(name)
            landed(from_twin.at[k], r0.at[k])
            arrived.add(name)

    def backward_sum(name, t):
        mine_sum = run[entry(bwd, rows_place.index(name) * 4 + t)]
        return mine_sum + from_twin[order.index(name), t].astype(F32)

    ups = [
        gather_up(rows_place, ready, backward_sum, staged_r, got_r, (sr, rr), c, sent)
        for c in range(2)
    ]
    for up in ups:
        next(up)
    for step in range(1, n_col):
        landed(gw_col.at[lax.rem(col + n_col - step, n_col)], r3.at[step])
    summed = gw_col[0]
    for c in range(1, n_col):
        summed = summed + gw_col[c]
    gw_mine = gw_all.at[pl.ds(row * 8, 8)]
    gw_all[pl.ds(row * 8, 8), :] = summed
    weights = [send(gw_mine, gw_mine, (s4, r4), step, row_peer(step)) for step in range(1, n_row)]
    for _ in range(2):
        for up in ups:
            next(up)
    for t in range(4):
        if t % 2 == 0:
            next(ups[t // 2])
        summed = gathered_tile(backward_sum, got_r, t) * back_factor[t]
        for b in range(8):
            out[pl.ds(t * 128 + b, 16, stride=8), :] = summed[b * 16 : (b + 1) * 16, :]
    for copy in sent:
        copy.wait_send()
    for copy in weights:
        copy.wait_send()
    for step in range(1, n_row):
        peer = lax.rem(row + n_row - step, n_row)
        landed(gw_all.at[pl.ds(peer * 8, 8)], r4.at[step])
    gw_out[...] = gw_all[...]


def hand_on_kernel(a, b, c, a_out, b_out, c_out):
    a_out[...] = a[...]
    b_out[...] = b[...]
    c_out[...] = c[...]


def spec(space=VMEM):
    return pl.BlockSpec(memory_space=space)


def shaped(shape, dtype):
    return jax.ShapeDtypeStruct(shape, dtype)


def remote_params(number):
    return pltpu.CompilerParams(
        collective_id=number, has_side_effects=True, vmem_limit_bytes=BIG
    )


def dma(count):
    return pltpu.SemaphoreType.DMA((count,))


def body(features, weight, degrees, tile_rows, tile_cols, tile_masks, cotangent):
    n_row = lax.axis_size("row")
    n_col = lax.axis_size("col")
    deg = degrees.reshape(n_row * n_col, 4, 128)
    rows = tile_rows.reshape(1, -1)
    cols = tile_cols.reshape(1, -1)
    masks = tile_masks.reshape(-1, 16, 128)
    hbm = spec(pl.ANY)
    n_rt, n_ct = 4 * n_col, 4 * n_row

    outs = (
        shaped((512, 256), BF16),
        shaped((512, 128), F32),
        shaped((128, 256), F32),
    )
    block = (4, 128, 128)
    results = pl.pallas_call(
        functools.partial(main_kernel, (512 * n_row * n_col) ** -0.5, n_row, n_col),
        out_shape=outs,
        in_specs=[spec(), spec(), spec(), hbm, spec(), hbm, spec()],
        out_specs=(spec(), spec(), spec()),
        scratch_shapes=[
            pltpu.SMEM((8, SLOTS), I32),
            pltpu.SMEM((8, SLOTS), I32),
            VMEM((8, SLOTS), I32),
            VMEM((8, SLOTS), I32),
            VMEM(block, F32),
            VMEM(block, F32),
            VMEM((4, 128), I32),
            VMEM((4, 128), I32),
            VMEM((n_ct, 128, 128), BF16),
            VMEM(block, BF16),
            VMEM((776, 16, 128), I32),
            VMEM((128, 128), F32),
            VMEM((EMPTY + 8, 128, 128), F32),
            VMEM((n_rt, 128, 128), BF16),
            VMEM(block, BF16),
            VMEM((7,) + block, BF16),
            VMEM((7,) + block, BF16),
            VMEM((8,) + block, BF16),
            VMEM((8,) + block, BF16),
            VMEM((7,) + block, BF16),
            VMEM((7,) + block, BF16),
            VMEM(block, F32),
            VMEM((4, 128, 256), F32),
            VMEM((128, 256), F32),
            VMEM((n_row, 8, 256), F32),
            VMEM((8, 256), F32),
            VMEM((n_col, 8, 256), F32),
            VMEM((128, 256), F32),
            dma(16),
            dma(16),
            dma(16),
            dma(16),
            dma(16),
            dma(16),
            dma(16),
            dma(16),
            dma(8),
            dma(8),
            dma(16),
            dma(16),
            dma(n_row),
            dma(n_row),
            dma(n_col),
            dma(n_col),
            dma(n_row),
            dma(n_row),
            pltpu.SemaphoreType.DMA,
            pltpu.SemaphoreType.DMA,
            dma(2),
            dma(2),
        ],
        compiler_params=remote_params(0),
        name="layer",
    )(rows, cols, features, masks, weight, deg, cotangent)
    return pl.pallas_call(
        hand_on_kernel,
        out_shape=outs,
        in_specs=[spec()] * 3,
        out_specs=(spec(), spec(), spec()),
        name="results",
    )(*results)


def solution(mesh):
    in_specs = (
        P(("col", "row"), None),
        P(),
        P(),
        P("row", "col", None),
        P("row", "col", None),
        P("row", "col", None, None, None),
        P(("row", "col"), None),
    )
    out_specs = (P(("row", "col"), None), P(("col", "row"), None), P())
    return jax.shard_map(body, mesh=mesh, in_specs=in_specs, out_specs=out_specs, check_vma=False)
```

```python
import functools

import jax
import jax.numpy as jnp
from jax import lax
from jax.experimental import pallas as pl
from jax.experimental.pallas import tpu as pltpu
from jax.sharding import PartitionSpec as P

F32 = jnp.float32
BF16 = jnp.bfloat16
I32 = jnp.int32
MESH = pl.DeviceIdType.MESH
VMEM = pltpu.VMEM
SLOTS = 1024
ROW_BITS = 5
COL_BITS = 6
CODE_BITS = ROW_BITS + COL_BITS
FRESH = 24
GROUP = 4
FWD_ROUNDS, FWD_UNROLL = 4, 54
BWD_ROUNDS, BWD_UNROLL = 4, 60
EMPTY = BWD_ROUNDS * BWD_UNROLL
BIG = 56 * 1024 * 1024


def mm(a, b):
    return jnp.dot(a, b, preferred_element_type=F32)


def iota(shape, dim):
    return lax.broadcasted_iota(I32, shape, dim)


def split(x):
    hi = x.astype(BF16)
    return hi, (x - hi.astype(F32)).astype(BF16)


class Place:
    def __init__(self, axis):
        self.axis = axis
        me = lax.axis_index(axis)
        if axis == "row":
            self.core = lax.rem(me, 2)
            chip = me // 2
        else:
            self.core = None
            chip = me
        self.p, self.q = chip // 4, lax.rem(chip, 4)

    def chip(self, name):
        p = 1 - self.p if name[0] == "x" else self.p
        turn = {"": 0, "m": 3, "p": 1, "2": 2}[name[1:]]
        return p * 4 + lax.rem(self.q + turn, 4)

    def index(self, name):
        chip = self.chip(name)
        return chip if self.core is None else chip * 2 + self.core

    def device(self, name):
        if name == "twin":
            return {self.axis: (self.p * 4 + self.q) * 2 + 1 - self.core}
        return {self.axis: self.index(name)}

    def partners(self):
        return ["x", "om", "op"] + ([] if self.core is None else ["twin"])


def send(src, dst, sems, i, device):
    copy = pltpu.make_async_remote_copy(
        src_ref=src,
        dst_ref=dst,
        send_sem=sems[0].at[i],
        recv_sem=sems[1].at[i],
        device_id=device,
        device_id_type=MESH,
    )
    copy.start()
    return copy


def landed(ref, sem):
    pltpu.make_async_copy(ref, ref, sem).wait()


class Place:
    def __init__(self, axis):
        self.axis = axis
        me = lax.axis_index(axis)
        if axis == "row":
            self.core = lax.rem(me, 2)
            chip = me // 2
        else:
            self.core = None
            chip = me
        self.p, self.q = chip // 4, lax.rem(chip, 4)

    def chip(self, name):
        p = 1 - self.p if name[0] == "x" else self.p
        turn = {"": 0, "m": 3, "p": 1, "2": 2}[name[1:]]
        return p * 4 + lax.rem(self.q + turn, 4)

    def index(self, name):
        chip = self.chip(name)
        return chip if self.core is None else chip * 2 + self.core

    def device(self, name):
        if name == "twin":
            return {self.axis: (self.p * 4 + self.q) * 2 + 1 - self.core}
        return {self.axis: self.index(name)}

def send(src, dst, sems, i, device):
    copy = pltpu.make_async_remote_copy(
        src_ref=src,
        dst_ref=dst,
        send_sem=sems[0].at[i],
        recv_sem=sems[1].at[i],
        device_id=device,
        device_id_type=MESH,
    )
    copy.start()
    return copy


def landed(ref, sem):
    pltpu.make_async_copy(ref, ref, sem).wait()


NAMES = ["x", "om", "op", "o2", "xm", "xp", "x2"]


ROUTES = (("x", "op"), ("x", "om"))
SOURCE = {"x": "o2", "op": "xm", "om": "xp"}


def together(*parts):
    for steps in zip(*parts):
        pass


def spread_start(place, mine, out, sems, twin_sems, chunk, sent):
    own = mine.at[pl.ds(2 * chunk, 2)]
    here = out.at[pl.ds(place.index("o") * 4 + 2 * chunk, 2)]
    for i, to in enumerate(("x", "op", "om")):
        sent.append(send(own, here, sems, 8 * chunk + i, place.device(to)))
    if place.core is not None:
        sent.append(send(own, here, twin_sems, 8 * chunk + 7, place.device("twin")))


def spread(place, out, sems, twin_sems, chunk, sent):
    low = 8 * chunk

    def part(index, first=0, tiles=2):
        return out.at[pl.ds(index * 4 + 2 * chunk + first, tiles)]

    def wait(i, name, first=0, tiles=2):
        landed(part(place.index(name), first, tiles), sems[1].at[low + i])

    def pass_on(i, to, name, first=0, tiles=2):
        ref = part(place.index(name), first, tiles)
        sent.append(send(ref, ref, sems, low + i, place.device(to)))

    def twin(*names):
        if place.core is not None:
            for name in names:
                ref = part(place.index(name))
                i = low + NAMES.index(name)
                sent.append(send(ref, ref, twin_sems, i, place.device("twin")))

    wait(0, "x")
    pass_on(3, "op", "x")
    wait(2, "op")
    pass_on(4, "x", "op")
    pass_on(5, "om", "op")
    wait(1, "om")
    yield
    wait(3, "xm")
    wait(4, "xp")
    wait(5, "o2")
    for t, to in enumerate(ROUTES[chunk]):
        pass_on(6 + t, to, SOURCE[to], t, 1)
    yield
    for t in range(2):
        wait(6 + t, "x2", t, 1)
    twin("x", "op", "om", "xm", "xp", "o2", "x2")
    yield
    if place.core is not None:
        for i, name in enumerate(NAMES + ["o"]):
            index = place.chip(name) * 2 + 1 - place.core
            landed(part(index), twin_sems[1].at[low + i])
    yield


def gather_up(place, ready, value, staged, got, sems, chunk, sent):
    low = 8 * chunk
    both = (2 * chunk, 2 * chunk + 1)

    def go(i, slot, into, to, tiles=both):
        at = pl.ds(tiles[0], len(tiles))
        sent.append(send(staged.at[slot, at], got.at[into, at], sems, low + i, place.device(to)))

    def wait(i, into, tiles=both):
        landed(got.at[into, pl.ds(tiles[0], len(tiles))], sems[1].at[low + i])

    def stage(name, slot, *added):
        ready(name)
        for t in both:
            total = value(name, t)
            for into, tiles in added:
                if t in tiles:
                    total = total + got[into, t].astype(F32)
            staged[slot, t] = total.astype(BF16)

    stage("x2", 0)
    go(0, 0, 0, "x", both[:1])
    go(1, 0, 0, ("om", "op")[chunk], both[1:])
    stage("om", 6)
    go(2, 6, 5, "om")
    yield
    if chunk == 0:
        stage("xp", 1)
        go(3, 1, 1, "x")
        wait(1, 0, both[1:])
        stage("xm", 2, (0, both[1:]))
        go(4, 2, 2, "om")
    else:
        stage("xm", 2)
        go(4, 2, 2, "om")
        wait(1, 0, both[1:])
        stage("xp", 1, (0, both[1:]))
        go(3, 1, 1, "x")
    wait(0, 0, both[:1])
    stage("o2", 3, (0, both[:1]))
    go(5, 3, 3, "op")
    yield
    wait(4, 2)
    stage("x", 4, (2, both))
    go(6, 4, 4, "x")
    wait(3, 1)
    wait(5, 3)
    stage("op", 5, (1, both), (3, both))
    go(7, 5, 6, "op")
    yield
    ready("o")
    for i, into in ((2, 5), (6, 4), (7, 6)):
        wait(i, into)
    yield


def gathered_tile(value, got, t):
    total = value("o", t)
    for i in (4, 5, 6):
        total = total + got[i, t].astype(F32)
    return total


def order_list(keys, rows, cols, n_keys, group):
    cap = keys.shape[1]
    hot = iota((n_keys, cap), 0) == keys
    hot_f = hot.astype(F32)
    upper = (iota((cap, cap), 0) < iota((cap, cap), 1)).astype(F32).astype(BF16)
    rank = mm(hot_f.astype(BF16), upper)
    count = jnp.sum(hot_f, axis=1, keepdims=True)
    groups = jnp.floor((count + (group - 1)) * (1.0 / group))
    wide = jnp.broadcast_to(groups, (n_keys, 128)).astype(BF16)
    lower = (iota((n_keys, n_keys), 1) < iota((n_keys, n_keys), 0)).astype(F32).astype(BF16)
    base = mm(lower, wide)[:, :1] * group
    pos = jnp.sum(hot_f * (rank + base), axis=0, keepdims=True)
    opens = jnp.sum(hot_f * rank, axis=0, keepdims=True) < 0.5
    place = (iota((SLOTS, cap), 0) == pos.astype(I32)).astype(F32).astype(BF16)
    which = iota((8, cap), 0)
    slot = iota((8, cap), 1)
    vals = jnp.where(
        which == 0,
        slot >> 4,
        jnp.where(
            which == 1,
            slot & 15,
            jnp.where(which == 2, cols, jnp.where(which == 3, rows, jnp.where(which == 4, 1, opens.astype(I32)))),
        ),
    )
    vals = vals.astype(F32).astype(BF16)
    found = lax.dot_general(vals, place, (((1,), (1,)), ((), ())), preferred_element_type=F32)
    f = found.astype(I32)
    code = ((f[0:1] * 16 + f[1:2]) << CODE_BITS) | (f[2:3] << ROW_BITS) | f[3:4]
    code = jnp.where(f[4:5] > 0, code, cap << CODE_BITS)
    code = code | (f[5:6] << FRESH)
    last = jnp.where(groups > 0.5, base * (1.0 / group) + groups - 1.0, 1.0 * EMPTY)
    square = (n_keys, SLOTS)
    last = jnp.sum(jnp.where(iota(square, 0) == iota(square, 1), last, 0.0), axis=0, keepdims=True)
    return jnp.where(iota((8, SLOTS), 0) == 0, code, last.astype(I32))


def scale_sources(feat, deg, mine):
    lane = iota((128, 128), 1)
    perm = (iota((128, 128), 0) == ((lane & 15) * 8 + (lane >> 4))).astype(F32).astype(BF16)
    degrees = mm(deg[...].astype(F32).astype(BF16), perm)
    bucket = iota((1, 128), 1) >> 4
    shrink = jnp.zeros((1, 128), F32)
    for b in range(8):
        shrink = jnp.where(bucket == b, 2.0**-b, shrink)
    inverse = lax.rsqrt(degrees)
    for t in range(4):
        turned = lax.dot_general(
            feat[t * 128 : (t + 1) * 128, :], perm, (((0,), (0,)), ((), ())), preferred_element_type=F32
        )
        factor = inverse[t : t + 1, :] * shrink
        mine[t] = (turned * factor).astype(BF16)
    return [inverse[t : t + 1, :] * shrink for t in range(4)]


def unpack(held, codes):
    words = jnp.concatenate([held[pl.ds(jnp.minimum((k >> CODE_BITS) & 1023, 768), 1)] for k in codes], axis=0)
    parts = [(words & (1 << b)).astype(F32).astype(BF16) for b in range(8)]
    return jnp.concatenate(parts, axis=1)


def entry(codes, key):
    return jnp.clip(codes[1, key], 0, EMPTY)


def run_tiles(start, stop, unroll, codes, product, acc, run):
    def body(i, carry):
        total = acc[...]
        for u in range(unroll):
            at = (i * unroll + u) * GROUP
            code = [codes[0, at + g] for g in range(GROUP)]
            keep = (1 - ((code[0] >> FRESH) & 1)).astype(F32)
            total = total * keep + product(code)
            run[i * unroll + u] = total
        acc[...] = total
        return carry

    lax.fori_loop(start, stop, body, 0)


def main_kernel(
    scale, n_row, n_col, rows_in, cols_in, feat_in, masks, weight_in, degrees_all, cot_in, act_out, out, gw_out,
    rows, cols, feat, weight, cot, act,
    fwd, bwd, fwd_list, bwd_list, out_factor, back_factor, deg_t, deg_s, src, source, held, acc, run, targets, mine, staged_c, got_c, twin_out, from_twin, staged_r, got_r,
    agg_hold, grad_hold, gw, gw_got, gw_row, gw_col, gw_all,
    sa, ra, st, rt, sc, rc, sg, rg, s0, r0, sr, rr, s2, r2, s3, r3, s4, r4, mask_sem, own_sem, deg_sem, list_sem,
):
    row = lax.axis_index("row")
    col = lax.axis_index("col")
    rows_place, cols_place = Place("row"), Place("col")
    load = pltpu.make_async_copy(masks, held.at[pl.ds(0, 768)], mask_sem)
    load.start()
    loads = [
        pltpu.make_async_copy(degrees_all.at[row * n_col + col], deg_t, deg_sem.at[0]),
        pltpu.make_async_copy(degrees_all.at[col * n_row + row], deg_s, deg_sem.at[1]),
    ]
    pairs = ((rows_in, rows), (cols_in, cols), (feat_in, feat), (weight_in, weight), (cot_in, cot))
    for i, (x, y) in enumerate(pairs):
        loads.append(pltpu.make_async_copy(x, y, deg_sem.at[2 + i]))
    for copy in loads:
        copy.start()
    barrier = pltpu.get_barrier_semaphore()

    def row_peer(step):
        return {"row": lax.rem(row + step, n_row)}

    def col_peer(step):
        return {"col": lax.rem(col + step, n_col)}

    for step in range(1, n_row):
        pl.semaphore_signal(barrier, inc=1, device_id=row_peer(step), device_id_type=MESH)
    for step in range(1, n_col):
        pl.semaphore_signal(barrier, inc=1, device_id=col_peer(step), device_id_type=MESH)
    held[768] = jnp.zeros((16, 128), I32)
    run[EMPTY] = jnp.zeros((128, 128), F32)
    for copy in loads:
        copy.wait()
    act_copy = pltpu.make_async_copy(act, act_out, deg_sem.at[7])
    back_factors = scale_sources(feat, deg_s, source)
    own = pltpu.make_async_copy(source, src.at[pl.ds(rows_place.index("o") * 4, 4)], own_sem)
    own.start()
    pl.semaphore_wait(barrier, n_row + n_col - 2)
    sent = []
    for c in range(2):
        spread_start(rows_place, source, src, (sa, ra), (st, rt), c, sent)
    r, c = rows[...], cols[...]
    fwd_list[...] = order_list(r, r, c, 1 << ROW_BITS, GROUP)
    bwd_list[...] = order_list(c, r, c, 1 << COL_BITS, GROUP)
    lists = [
        pltpu.make_async_copy(fwd_list, fwd, list_sem.at[0]),
        pltpu.make_async_copy(bwd_list, bwd, list_sem.at[1]),
    ]
    for copy in lists:
        copy.start()
    inverse = lax.rsqrt(deg_t[...].astype(F32))
    for t in range(4):
        back_factor[t] = jnp.broadcast_to(back_factors[t], (128, 128)).T
        out_factor[t] = jnp.broadcast_to(inverse[t : t + 1, :], (128, 128)).T
    own.wait()
    together(*[spread(rows_place, src, (sa, ra), (st, rt), c, sent) for c in range(2)])
    load.wait()
    for copy in lists:
        copy.wait()

    def forward(code):
        lhs = jnp.concatenate(
            [src[(k >> ROW_BITS) & ((1 << COL_BITS) - 1)] for k in code], axis=1
        )
        return mm(lhs, unpack(held, code).reshape(GROUP * 128, 128))

    acc[...] = jnp.zeros_like(acc)
    run_tiles(0, FWD_ROUNDS, FWD_UNROLL, fwd, forward, acc, run)

    def forward_sum(name, t):
        return run[entry(fwd, cols_place.index(name) * 4 + t)]

    ups = [
        gather_up(cols_place, lambda name: None, forward_sum, staged_c, got_c, (sc, rc), c, sent)
        for c in range(2)
    ]
    for _ in range(3):
        for up in ups:
            next(up)
    w = weight[...]
    for c in range(2):
        next(ups[c])
        for t in (2 * c, 2 * c + 1):
            summed = gathered_tile(forward_sum, got_c, t)
            agg_t = summed * inverse[t : t + 1, :]
            factor = out_factor[t]
            factor = jnp.concatenate([factor, factor], axis=1)
            hi, lo = split(agg_t.T)
            pre = mm(hi, w) + mm(lo, w)
            slope = jnp.where(pre > 0, 1.0, jnp.exp(jnp.minimum(pre, 0.0)))
            here = pl.ds(t * 128, 128)
            act[here, :] = jnp.where(pre > 0, pre, slope - 1.0).astype(BF16)
            grad = cot[here, :].astype(F32) * slope
            agg_hold[t] = agg_t
            grad_hold[t] = grad
            scaled = (grad * factor).astype(BF16)
            mine[t] = lax.dot_general(
                scaled, w, (((1,), (1,)), ((), ())), preferred_element_type=F32
            ).astype(BF16)
        spread_start(cols_place, mine, targets, (sg, rg), None, c, sent)
    own = pltpu.make_async_copy(mine, targets.at[pl.ds(col * 4, 4)], own_sem)
    own.start()
    act_copy.start()
    total = jnp.zeros((128, 256), F32)
    for t in range(4):
        t_hi, t_lo = split(agg_hold[t])
        g_hi, g_lo = split(grad_hold[t])
        total = total + (mm(t_hi, g_hi) + (mm(t_lo, g_hi) + mm(t_hi, g_lo)))
    gw[...] = total * scale
    own.wait()
    together(*[spread(cols_place, targets, (sg, rg), None, c, sent) for c in range(2)])
    weights = [
        send(
            gw.at[pl.ds(lax.rem(row + step, n_row) * 8, 8)],
            gw_got.at[step],
            (s2, r2),
            step,
            row_peer(step),
        )
        for step in range(1, n_row)
    ]

    def backward(code):
        rhs = jnp.concatenate([targets[k & ((1 << ROW_BITS) - 1)] for k in code], axis=0)
        tiles = unpack(held, code)
        return mm(jnp.concatenate([tiles[g] for g in range(GROUP)], axis=1), rhs)

    acc[...] = jnp.zeros_like(acc)
    run_tiles(0, BWD_ROUNDS // 2, BWD_UNROLL, bwd, backward, acc, run)
    for copy in weights:
        copy.wait()
    summed = gw[pl.ds(row * 8, 8), :]
    for step in range(1, n_row):
        summed = summed + gw_got[step]
    gw_row[...] = summed
    gw_col[pl.ds(col, 1)] = summed[None]
    for step in range(1, n_col):
        sent.append(send(gw_row, gw_col.at[col], (s3, r3), step, col_peer(step)))
    run_tiles(BWD_ROUNDS // 2, BWD_ROUNDS, BWD_UNROLL, bwd, backward, acc, run)

    order = ["x2", "om", "xp", "xm", "o2", "x", "op", "o"]
    for k, name in enumerate(order):
        index = rows_place.chip(name) * 2 + 1 - rows_place.core
        for t in range(4):
            twin_out[k, t] = run[entry(bwd, index * 4 + t)].astype(BF16)
        sent.append(
            send(twin_out.at[k], from_twin.at[k], (s0, r0), k, rows_place.device("twin"))
        )
    arrived = set()

    def ready(name):
        if name not in arrived:
            k = order.index(name)
            landed(from_twin.at[k], r0.at[k])
            arrived.add(name)

    def backward_sum(name, t):
        mine_sum = run[entry(bwd, rows_place.index(name) * 4 + t)]
        return mine_sum + from_twin[order.index(name), t].astype(F32)

    ups = [
        gather_up(rows_place, ready, backward_sum, staged_r, got_r, (sr, rr), c, sent)
        for c in range(2)
    ]
    for up in ups:
        next(up)
    for step in range(1, n_col):
        landed(gw_col.at[lax.rem(col + n_col - step, n_col)], r3.at[step])
    summed = gw_col[0]
    for c in range(1, n_col):
        summed = summed + gw_col[c]
    gw_mine = gw_all.at[pl.ds(row * 8, 8)]
    gw_all[pl.ds(row * 8, 8), :] = summed
    weights = [send(gw_mine, gw_mine, (s4, r4), step, row_peer(step)) for step in range(1, n_row)]
    for _ in range(2):
        for up in ups:
            next(up)
    for t in range(4):
        if t % 2 == 0:
            next(ups[t // 2])
        summed = gathered_tile(backward_sum, got_r, t) * back_factor[t]
        for b in range(8):
            out[pl.ds(t * 128 + b, 16, stride=8), :] = summed[b * 16 : (b + 1) * 16, :]
    for copy in sent:
        copy.wait_send()
    for copy in weights:
        copy.wait_send()
    for step in range(1, n_row):
        peer = lax.rem(row + n_row - step, n_row)
        landed(gw_all.at[pl.ds(peer * 8, 8)], r4.at[step])
    act_copy.wait()
    gw_out[...] = gw_all[...]


def hand_on_kernel(a, b, c, a_out, b_out, c_out):
    a_out[...] = a[...]
    b_out[...] = b[...]
    c_out[...] = c[...]


def spec(space=VMEM):
    return pl.BlockSpec(memory_space=space)


def shaped(shape, dtype):
    return jax.ShapeDtypeStruct(shape, dtype)


def remote_params(number):
    return pltpu.CompilerParams(
        collective_id=number, has_side_effects=True, vmem_limit_bytes=BIG
    )


def dma(count):
    return pltpu.SemaphoreType.DMA((count,))


def body(features, weight, degrees, tile_rows, tile_cols, tile_masks, cotangent):
    n_row = lax.axis_size("row")
    n_col = lax.axis_size("col")
    deg = degrees.reshape(n_row * n_col, 4, 128)
    rows = tile_rows.reshape(1, -1)
    cols = tile_cols.reshape(1, -1)
    masks = tile_masks.reshape(-1, 16, 128)
    hbm = spec(pl.ANY)
    n_rt, n_ct = 4 * n_col, 4 * n_row

    outs = (
        shaped((512, 256), BF16),
        shaped((512, 128), F32),
        shaped((128, 256), F32),
    )
    block = (4, 128, 128)
    results = pl.pallas_call(
        functools.partial(main_kernel, (512 * n_row * n_col) ** -0.5, n_row, n_col),
        out_shape=outs,
        in_specs=[hbm] * 7,
        out_specs=(hbm, spec(), spec()),
        scratch_shapes=[
            VMEM(rows.shape, I32),
            VMEM(cols.shape, I32),
            VMEM(features.shape, BF16),
            VMEM(weight.shape, BF16),
            VMEM(cotangent.shape, BF16),
            VMEM(cotangent.shape, BF16),
            pltpu.SMEM((8, SLOTS), I32),
            pltpu.SMEM((8, SLOTS), I32),
            VMEM((8, SLOTS), I32),
            VMEM((8, SLOTS), I32),
            VMEM(block, F32),
            VMEM(block, F32),
            VMEM((4, 128), I32),
            VMEM((4, 128), I32),
            VMEM((n_ct, 128, 128), BF16),
            VMEM(block, BF16),
            VMEM((776, 16, 128), I32),
            VMEM((128, 128), F32),
            VMEM((EMPTY + 8, 128, 128), F32),
            VMEM((n_rt, 128, 128), BF16),
            VMEM(block, BF16),
            VMEM((7,) + block, BF16),
            VMEM((7,) + block, BF16),
            VMEM((8,) + block, BF16),
            VMEM((8,) + block, BF16),
            VMEM((7,) + block, BF16),
            VMEM((7,) + block, BF16),
            VMEM(block, F32),
            VMEM((4, 128, 256), F32),
            VMEM((128, 256), F32),
            VMEM((n_row, 8, 256), F32),
            VMEM((8, 256), F32),
            VMEM((n_col, 8, 256), F32),
            VMEM((128, 256), F32),
            dma(16),
            dma(16),
            dma(16),
            dma(16),
            dma(16),
            dma(16),
            dma(16),
            dma(16),
            dma(8),
            dma(8),
            dma(16),
            dma(16),
            dma(n_row),
            dma(n_row),
            dma(n_col),
            dma(n_col),
            dma(n_row),
            dma(n_row),
            pltpu.SemaphoreType.DMA,
            pltpu.SemaphoreType.DMA,
            dma(8),
            dma(2),
        ],
        compiler_params=remote_params(0),
        name="layer",
    )(rows, cols, features, masks, weight, deg, cotangent)
    return pl.pallas_call(
        hand_on_kernel,
        out_shape=outs,
        in_specs=[spec()] * 3,
        out_specs=(spec(), spec(), spec()),
        name="results",
    )(*results)


def solution(mesh):
    in_specs = (
        P(("col", "row"), None),
        P(),
        P(),
        P("row", "col", None),
        P("row", "col", None),
        P("row", "col", None, None, None),
        P(("row", "col"), None),
    )
    out_specs = (P(("row", "col"), None), P(("col", "row"), None), P())
    return jax.shard_map(body, mesh=mesh, in_specs=in_specs, out_specs=out_specs, check_vma=False)
```

```python
import functools

import jax
import jax.numpy as jnp
from jax import lax
from jax.experimental import pallas as pl
from jax.experimental.pallas import tpu as pltpu
from jax.sharding import PartitionSpec as P

F32 = jnp.float32
BF16 = jnp.bfloat16
I32 = jnp.int32
MESH = pl.DeviceIdType.MESH
VMEM = pltpu.VMEM
SLOTS = 1024
ROW_BITS = 5
COL_BITS = 6
CODE_BITS = ROW_BITS + COL_BITS
FRESH = 24
GROUP = 4
FWD_ROUNDS, FWD_UNROLL = 4, 54
BWD_ROUNDS, BWD_UNROLL = 4, 60
EMPTY = BWD_ROUNDS * BWD_UNROLL
BIG = 56 * 1024 * 1024


def mm(a, b):
    return jnp.dot(a, b, preferred_element_type=F32)


def iota(shape, dim):
    return lax.broadcasted_iota(I32, shape, dim)


def split(x):
    hi = x.astype(BF16)
    return hi, (x - hi.astype(F32)).astype(BF16)


class Place:
    def __init__(self, axis):
        self.axis = axis
        me = lax.axis_index(axis)
        if axis == "row":
            self.core = lax.rem(me, 2)
            chip = me // 2
        else:
            self.core = None
            chip = me
        self.p, self.q = chip // 4, lax.rem(chip, 4)

    def chip(self, name):
        p = 1 - self.p if name[0] == "x" else self.p
        turn = {"": 0, "m": 3, "p": 1, "2": 2}[name[1:]]
        return p * 4 + lax.rem(self.q + turn, 4)

    def index(self, name):
        chip = self.chip(name)
        return chip if self.core is None else chip * 2 + self.core

    def device(self, name):
        if name == "twin":
            return {self.axis: (self.p * 4 + self.q) * 2 + 1 - self.core}
        return {self.axis: self.index(name)}

    def partners(self):
        return ["x", "om", "op"] + ([] if self.core is None else ["twin"])


def send(src, dst, sems, i, device):
    copy = pltpu.make_async_remote_copy(
        src_ref=src,
        dst_ref=dst,
        send_sem=sems[0].at[i],
        recv_sem=sems[1].at[i],
        device_id=device,
        device_id_type=MESH,
    )
    copy.start()
    return copy


def landed(ref, sem):
    pltpu.make_async_copy(ref, ref, sem).wait()


class Place:
    def __init__(self, axis):
        self.axis = axis
        me = lax.axis_index(axis)
        if axis == "row":
            self.core = lax.rem(me, 2)
            chip = me // 2
        else:
            self.core = None
            chip = me
        self.p, self.q = chip // 4, lax.rem(chip, 4)

    def chip(self, name):
        p = 1 - self.p if name[0] == "x" else self.p
        turn = {"": 0, "m": 3, "p": 1, "2": 2}[name[1:]]
        return p * 4 + lax.rem(self.q + turn, 4)

    def index(self, name):
        chip = self.chip(name)
        return chip if self.core is None else chip * 2 + self.core

    def device(self, name):
        if name == "twin":
            return {self.axis: (self.p * 4 + self.q) * 2 + 1 - self.core}
        return {self.axis: self.index(name)}

def send(src, dst, sems, i, device):
    copy = pltpu.make_async_remote_copy(
        src_ref=src,
        dst_ref=dst,
        send_sem=sems[0].at[i],
        recv_sem=sems[1].at[i],
        device_id=device,
        device_id_type=MESH,
    )
    copy.start()
    return copy


def landed(ref, sem):
    pltpu.make_async_copy(ref, ref, sem).wait()


NAMES = ["x", "om", "op", "o2", "xm", "xp", "x2"]


ROUTES = (("x", "op"), ("x", "om"))
SOURCE = {"x": "o2", "op": "xm", "om": "xp"}


def together(*parts):
    for steps in zip(*parts):
        pass


def spread_start(place, mine, out, sems, twin_sems, chunk, sent):
    own = mine.at[pl.ds(2 * chunk, 2)]
    here = out.at[pl.ds(place.index("o") * 4 + 2 * chunk, 2)]
    for i, to in ((1, "op"), (2, "om"), (0, "x")):
        sent.append(send(own, here, sems, 8 * chunk + i, place.device(to)))
    if place.core is not None:
        sent.append(send(own, here, twin_sems, 8 * chunk + 7, place.device("twin")))


def spread(place, out, sems, twin_sems, chunk, sent):
    low = 8 * chunk

    def part(index, first=0, tiles=2):
        return out.at[pl.ds(index * 4 + 2 * chunk + first, tiles)]

    def wait(i, name, first=0, tiles=2):
        landed(part(place.index(name), first, tiles), sems[1].at[low + i])

    def pass_on(i, to, name, first=0, tiles=2):
        ref = part(place.index(name), first, tiles)
        sent.append(send(ref, ref, sems, low + i, place.device(to)))

    def twin(*names):
        if place.core is not None:
            for name in names:
                ref = part(place.index(name))
                i = low + NAMES.index(name)
                sent.append(send(ref, ref, twin_sems, i, place.device("twin")))

    wait(0, "x")
    pass_on(3, "op", "x")
    wait(2, "op")
    pass_on(4, "x", "op")
    pass_on(5, "om", "op")
    yield
    for t, to in reversed(list(enumerate(ROUTES[chunk]))):
        name = SOURCE[to]
        wait({"xm": 3, "xp": 4, "o2": 5}[name], name)
        pass_on(6 + t, to, name, t, 1)
    yield
    wait(1, "om")
    wait(*((4, "xp") if chunk == 0 else (3, "xm")))
    for t in range(2):
        wait(6 + t, "x2", t, 1)
    twin("x", "op", "om", "xm", "xp", "o2", "x2")
    yield
    if place.core is not None:
        for i, name in enumerate(NAMES + ["o"]):
            index = place.chip(name) * 2 + 1 - place.core
            landed(part(index), twin_sems[1].at[low + i])
    yield


def gather_up(place, ready, value, staged, got, sems, chunk, sent):
    low = 8 * chunk
    both = (2 * chunk, 2 * chunk + 1)

    def go(i, slot, into, to, tiles=both):
        at = pl.ds(tiles[0], len(tiles))
        sent.append(send(staged.at[slot, at], got.at[into, at], sems, low + i, place.device(to)))

    def wait(i, into, tiles=both):
        landed(got.at[into, pl.ds(tiles[0], len(tiles))], sems[1].at[low + i])

    def stage(name, slot, *added):
        ready(name)
        for t in both:
            total = value(name, t)
            for into, tiles in added:
                if t in tiles:
                    total = total + got[into, t].astype(F32)
            staged[slot, t] = total.astype(BF16)

    stage("x2", 0)
    go(0, 0, 0, "x", both[:1])
    go(1, 0, 0, ("om", "op")[chunk], both[1:])
    stage("om", 6)
    go(2, 6, 5, "om")
    yield
    if chunk == 0:
        stage("xp", 1)
        go(3, 1, 1, "x")
        wait(1, 0, both[1:])
        stage("xm", 2, (0, both[1:]))
        go(4, 2, 2, "om")
    else:
        stage("xm", 2)
        go(4, 2, 2, "om")
        wait(1, 0, both[1:])
        stage("xp", 1, (0, both[1:]))
        go(3, 1, 1, "x")
    wait(0, 0, both[:1])
    stage("o2", 3, (0, both[:1]))
    go(5, 3, 3, "op")
    yield
    wait(4, 2)
    stage("x", 4, (2, both))
    go(6, 4, 4, "x")
    wait(3, 1)
    wait(5, 3)
    stage("op", 5, (1, both), (3, both))
    go(7, 5, 6, "op")
    yield
    ready("o")
    for i, into in ((2, 5), (6, 4), (7, 6)):
        wait(i, into)
    yield


def gathered_tile(value, got, t):
    total = value("o", t)
    for i in (4, 5, 6):
        total = total + got[i, t].astype(F32)
    return total


def order_list(keys, rows, cols, n_keys, group):
    cap = keys.shape[1]
    hot = iota((n_keys, cap), 0) == keys
    hot_f = hot.astype(F32)
    upper = (iota((cap, cap), 0) < iota((cap, cap), 1)).astype(F32).astype(BF16)
    rank = mm(hot_f.astype(BF16), upper)
    count = jnp.sum(hot_f, axis=1, keepdims=True)
    groups = jnp.floor((count + (group - 1)) * (1.0 / group))
    wide = jnp.broadcast_to(groups, (n_keys, 128)).astype(BF16)
    lower = (iota((n_keys, n_keys), 1) < iota((n_keys, n_keys), 0)).astype(F32).astype(BF16)
    base = mm(lower, wide)[:, :1] * group
    pos = jnp.sum(hot_f * (rank + base), axis=0, keepdims=True)
    opens = jnp.sum(hot_f * rank, axis=0, keepdims=True) < 0.5
    place = (iota((SLOTS, cap), 0) == pos.astype(I32)).astype(F32).astype(BF16)
    which = iota((8, cap), 0)
    slot = iota((8, cap), 1)
    vals = jnp.where(
        which == 0,
        slot >> 4,
        jnp.where(
            which == 1,
            slot & 15,
            jnp.where(which == 2, cols, jnp.where(which == 3, rows, jnp.where(which == 4, 1, opens.astype(I32)))),
        ),
    )
    vals = vals.astype(F32).astype(BF16)
    found = lax.dot_general(vals, place, (((1,), (1,)), ((), ())), preferred_element_type=F32)
    f = found.astype(I32)
    code = ((f[0:1] * 16 + f[1:2]) << CODE_BITS) | (f[2:3] << ROW_BITS) | f[3:4]
    code = jnp.where(f[4:5] > 0, code, cap << CODE_BITS)
    code = code | (f[5:6] << FRESH)
    last = jnp.where(groups > 0.5, base * (1.0 / group) + groups - 1.0, 1.0 * EMPTY)
    square = (n_keys, SLOTS)
    last = jnp.sum(jnp.where(iota(square, 0) == iota(square, 1), last, 0.0), axis=0, keepdims=True)
    return jnp.where(iota((8, SLOTS), 0) == 0, code, last.astype(I32))


def scale_sources(feat, deg, mine):
    lane = iota((128, 128), 1)
    perm = (iota((128, 128), 0) == ((lane & 15) * 8 + (lane >> 4))).astype(F32).astype(BF16)
    degrees = mm(deg[...].astype(F32).astype(BF16), perm)
    bucket = iota((1, 128), 1) >> 4
    shrink = jnp.zeros((1, 128), F32)
    for b in range(8):
        shrink = jnp.where(bucket == b, 2.0**-b, shrink)
    inverse = lax.rsqrt(degrees)
    for t in range(4):
        turned = lax.dot_general(
            feat[t * 128 : (t + 1) * 128, :], perm, (((0,), (0,)), ((), ())), preferred_element_type=F32
        )
        factor = inverse[t : t + 1, :] * shrink
        mine[t] = (turned * factor).astype(BF16)
    return [inverse[t : t + 1, :] * shrink for t in range(4)]


def unpack(held, codes):
    words = jnp.concatenate([held[pl.ds(jnp.minimum((k >> CODE_BITS) & 1023, 768), 1)] for k in codes], axis=0)
    parts = [(words & (1 << b)).astype(F32).astype(BF16) for b in range(8)]
    return jnp.concatenate(parts, axis=1)


def entry(codes, key):
    return jnp.clip(codes[1, key], 0, EMPTY)


def run_tiles(start, stop, unroll, codes, product, acc, run):
    def body(i, carry):
        total = acc[...]
        for u in range(unroll):
            at = (i * unroll + u) * GROUP
            code = [codes[0, at + g] for g in range(GROUP)]
            keep = (1 - ((code[0] >> FRESH) & 1)).astype(F32)
            total = total * keep + product(code)
            run[i * unroll + u] = total
        acc[...] = total
        return carry

    lax.fori_loop(start, stop, body, 0)


def main_kernel(
    scale, n_row, n_col, rows_in, cols_in, feat_in, masks, weight_in, degrees_all, cot_in, act_out, out, gw_out,
    rows, cols, feat, weight, cot, act,
    fwd, bwd, fwd_list, bwd_list, out_factor, back_factor, deg_t, deg_s, src, source, held, acc, run, targets, mine, staged_c, got_c, twin_out, from_twin, staged_r, got_r,
    agg_hold, grad_hold, gw, gw_got, gw_row, gw_col, gw_all,
    sa, ra, st, rt, sc, rc, sg, rg, s0, r0, sr, rr, s2, r2, s3, r3, s4, r4, mask_sem, own_sem, deg_sem, list_sem,
):
    row = lax.axis_index("row")
    col = lax.axis_index("col")
    rows_place, cols_place = Place("row"), Place("col")
    load = pltpu.make_async_copy(masks, held.at[pl.ds(0, 768)], mask_sem)
    load.start()
    loads = [
        pltpu.make_async_copy(degrees_all.at[row * n_col + col], deg_t, deg_sem.at[0]),
        pltpu.make_async_copy(degrees_all.at[col * n_row + row], deg_s, deg_sem.at[1]),
    ]
    pairs = ((rows_in, rows), (cols_in, cols), (feat_in, feat), (weight_in, weight), (cot_in, cot))
    for i, (x, y) in enumerate(pairs):
        loads.append(pltpu.make_async_copy(x, y, deg_sem.at[2 + i]))
    for copy in loads:
        copy.start()
    barrier = pltpu.get_barrier_semaphore()

    def row_peer(step):
        return {"row": lax.rem(row + step, n_row)}

    def col_peer(step):
        return {"col": lax.rem(col + step, n_col)}

    for step in range(1, n_row):
        pl.semaphore_signal(barrier, inc=1, device_id=row_peer(step), device_id_type=MESH)
    for step in range(1, n_col):
        pl.semaphore_signal(barrier, inc=1, device_id=col_peer(step), device_id_type=MESH)
    held[768] = jnp.zeros((16, 128), I32)
    run[EMPTY] = jnp.zeros((128, 128), F32)
    for copy in loads:
        copy.wait()
    act_copy = pltpu.make_async_copy(act, act_out, deg_sem.at[7])
    back_factors = scale_sources(feat, deg_s, source)
    own = pltpu.make_async_copy(source, src.at[pl.ds(rows_place.index("o") * 4, 4)], own_sem)
    own.start()
    pl.semaphore_wait(barrier, n_row + n_col - 2)
    sent = []
    for c in range(2):
        spread_start(rows_place, source, src, (sa, ra), (st, rt), c, sent)
    r, c = rows[...], cols[...]
    fwd_list[...] = order_list(r, r, c, 1 << ROW_BITS, GROUP)
    bwd_list[...] = order_list(c, r, c, 1 << COL_BITS, GROUP)
    lists = [
        pltpu.make_async_copy(fwd_list, fwd, list_sem.at[0]),
        pltpu.make_async_copy(bwd_list, bwd, list_sem.at[1]),
    ]
    for copy in lists:
        copy.start()
    inverse = lax.rsqrt(deg_t[...].astype(F32))
    for t in range(4):
        back_factor[t] = jnp.broadcast_to(back_factors[t], (128, 128)).T
        out_factor[t] = jnp.broadcast_to(inverse[t : t + 1, :], (128, 128)).T
    own.wait()
    together(*[spread(rows_place, src, (sa, ra), (st, rt), c, sent) for c in range(2)])
    load.wait()
    for copy in lists:
        copy.wait()

    def forward(code):
        lhs = jnp.concatenate(
            [src[(k >> ROW_BITS) & ((1 << COL_BITS) - 1)] for k in code], axis=1
        )
        return mm(lhs, unpack(held, code).reshape(GROUP * 128, 128))

    acc[...] = jnp.zeros_like(acc)
    run_tiles(0, FWD_ROUNDS, FWD_UNROLL, fwd, forward, acc, run)

    def forward_sum(name, t):
        return run[entry(fwd, cols_place.index(name) * 4 + t)]

    ups = [
        gather_up(cols_place, lambda name: None, forward_sum, staged_c, got_c, (sc, rc), c, sent)
        for c in range(2)
    ]
    for _ in range(3):
        for up in ups:
            next(up)
    w = weight[...]
    for c in range(2):
        next(ups[c])
        for t in (2 * c, 2 * c + 1):
            summed = gathered_tile(forward_sum, got_c, t)
            agg_t = summed * inverse[t : t + 1, :]
            factor = out_factor[t]
            factor = jnp.concatenate([factor, factor], axis=1)
            hi, lo = split(agg_t.T)
            pre = mm(hi, w) + mm(lo, w)
            slope = jnp.where(pre > 0, 1.0, jnp.exp(jnp.minimum(pre, 0.0)))
            here = pl.ds(t * 128, 128)
            act[here, :] = jnp.where(pre > 0, pre, slope - 1.0).astype(BF16)
            grad = cot[here, :].astype(F32) * slope
            agg_hold[t] = agg_t
            grad_hold[t] = grad
            scaled = (grad * factor).astype(BF16)
            mine[t] = lax.dot_general(
                scaled, w, (((1,), (1,)), ((), ())), preferred_element_type=F32
            ).astype(BF16)
        spread_start(cols_place, mine, targets, (sg, rg), None, c, sent)
    own = pltpu.make_async_copy(mine, targets.at[pl.ds(col * 4, 4)], own_sem)
    own.start()
    act_copy.start()
    total = jnp.zeros((128, 256), F32)
    for t in range(4):
        t_hi, t_lo = split(agg_hold[t])
        g_hi, g_lo = split(grad_hold[t])
        total = total + (mm(t_hi, g_hi) + (mm(t_lo, g_hi) + mm(t_hi, g_lo)))
    gw[...] = total * scale
    own.wait()
    together(*[spread(cols_place, targets, (sg, rg), None, c, sent) for c in range(2)])
    weights = [
        send(
            gw.at[pl.ds(lax.rem(row + step, n_row) * 8, 8)],
            gw_got.at[step],
            (s2, r2),
            step,
            row_peer(step),
        )
        for step in range(1, n_row)
    ]

    def backward(code):
        rhs = jnp.concatenate([targets[k & ((1 << ROW_BITS) - 1)] for k in code], axis=0)
        tiles = unpack(held, code)
        return mm(jnp.concatenate([tiles[g] for g in range(GROUP)], axis=1), rhs)

    acc[...] = jnp.zeros_like(acc)
    run_tiles(0, BWD_ROUNDS // 2, BWD_UNROLL, bwd, backward, acc, run)
    for copy in weights:
        copy.wait()
    summed = gw[pl.ds(row * 8, 8), :]
    for step in range(1, n_row):
        summed = summed + gw_got[step]
    gw_row[...] = summed
    gw_col[pl.ds(col, 1)] = summed[None]
    for step in range(1, n_col):
        sent.append(send(gw_row, gw_col.at[col], (s3, r3), step, col_peer(step)))
    run_tiles(BWD_ROUNDS // 2, BWD_ROUNDS, BWD_UNROLL, bwd, backward, acc, run)

    order = ["x2", "om", "xp", "xm", "o2", "x", "op", "o"]
    for k, name in enumerate(order):
        index = rows_place.chip(name) * 2 + 1 - rows_place.core
        for t in range(4):
            twin_out[k, t] = run[entry(bwd, index * 4 + t)].astype(BF16)
        sent.append(
            send(twin_out.at[k], from_twin.at[k], (s0, r0), k, rows_place.device("twin"))
        )
    arrived = set()

    def ready(name):
        if name not in arrived:
            k = order.index(name)
            landed(from_twin.at[k], r0.at[k])
            arrived.add(name)

    def backward_sum(name, t):
        mine_sum = run[entry(bwd, rows_place.index(name) * 4 + t)]
        return mine_sum + from_twin[order.index(name), t].astype(F32)

    ups = [
        gather_up(rows_place, ready, backward_sum, staged_r, got_r, (sr, rr), c, sent)
        for c in range(2)
    ]
    for up in ups:
        next(up)
    for step in range(1, n_col):
        landed(gw_col.at[lax.rem(col + n_col - step, n_col)], r3.at[step])
    summed = gw_col[0]
    for c in range(1, n_col):
        summed = summed + gw_col[c]
    gw_mine = gw_all.at[pl.ds(row * 8, 8)]
    gw_all[pl.ds(row * 8, 8), :] = summed
    weights = [send(gw_mine, gw_mine, (s4, r4), step, row_peer(step)) for step in range(1, n_row)]
    for _ in range(2):
        for up in ups:
            next(up)
    for t in range(4):
        if t % 2 == 0:
            next(ups[t // 2])
        summed = gathered_tile(backward_sum, got_r, t) * back_factor[t]
        for b in range(8):
            out[pl.ds(t * 128 + b, 16, stride=8), :] = summed[b * 16 : (b + 1) * 16, :]
    for copy in sent:
        copy.wait_send()
    for copy in weights:
        copy.wait_send()
    for step in range(1, n_row):
        peer = lax.rem(row + n_row - step, n_row)
        landed(gw_all.at[pl.ds(peer * 8, 8)], r4.at[step])
    act_copy.wait()
    gw_out[...] = gw_all[...]


def hand_on_kernel(a, b, c, a_out, b_out, c_out):
    a_out[...] = a[...]
    b_out[...] = b[...]
    c_out[...] = c[...]


def spec(space=VMEM):
    return pl.BlockSpec(memory_space=space)


def shaped(shape, dtype):
    return jax.ShapeDtypeStruct(shape, dtype)


def remote_params(number):
    return pltpu.CompilerParams(
        collective_id=number, has_side_effects=True, vmem_limit_bytes=BIG
    )


def dma(count):
    return pltpu.SemaphoreType.DMA((count,))


def body(features, weight, degrees, tile_rows, tile_cols, tile_masks, cotangent):
    n_row = lax.axis_size("row")
    n_col = lax.axis_size("col")
    deg = degrees.reshape(n_row * n_col, 4, 128)
    rows = tile_rows.reshape(1, -1)
    cols = tile_cols.reshape(1, -1)
    masks = tile_masks.reshape(-1, 16, 128)
    hbm = spec(pl.ANY)
    n_rt, n_ct = 4 * n_col, 4 * n_row

    outs = (
        shaped((512, 256), BF16),
        shaped((512, 128), F32),
        shaped((128, 256), F32),
    )
    block = (4, 128, 128)
    results = pl.pallas_call(
        functools.partial(main_kernel, (512 * n_row * n_col) ** -0.5, n_row, n_col),
        out_shape=outs,
        in_specs=[hbm] * 7,
        out_specs=(hbm, spec(), spec()),
        scratch_shapes=[
            VMEM(rows.shape, I32),
            VMEM(cols.shape, I32),
            VMEM(features.shape, BF16),
            VMEM(weight.shape, BF16),
            VMEM(cotangent.shape, BF16),
            VMEM(cotangent.shape, BF16),
            pltpu.SMEM((8, SLOTS), I32),
            pltpu.SMEM((8, SLOTS), I32),
            VMEM((8, SLOTS), I32),
            VMEM((8, SLOTS), I32),
            VMEM(block, F32),
            VMEM(block, F32),
            VMEM((4, 128), I32),
            VMEM((4, 128), I32),
            VMEM((n_ct, 128, 128), BF16),
            VMEM(block, BF16),
            VMEM((776, 16, 128), I32),
            VMEM((128, 128), F32),
            VMEM((EMPTY + 8, 128, 128), F32),
            VMEM((n_rt, 128, 128), BF16),
            VMEM(block, BF16),
            VMEM((7,) + block, BF16),
            VMEM((7,) + block, BF16),
            VMEM((8,) + block, BF16),
            VMEM((8,) + block, BF16),
            VMEM((7,) + block, BF16),
            VMEM((7,) + block, BF16),
            VMEM(block, F32),
            VMEM((4, 128, 256), F32),
            VMEM((128, 256), F32),
            VMEM((n_row, 8, 256), F32),
            VMEM((8, 256), F32),
            VMEM((n_col, 8, 256), F32),
            VMEM((128, 256), F32),
            dma(16),
            dma(16),
            dma(16),
            dma(16),
            dma(16),
            dma(16),
            dma(16),
            dma(16),
            dma(8),
            dma(8),
            dma(16),
            dma(16),
            dma(n_row),
            dma(n_row),
            dma(n_col),
            dma(n_col),
            dma(n_row),
            dma(n_row),
            pltpu.SemaphoreType.DMA,
            pltpu.SemaphoreType.DMA,
            dma(8),
            dma(2),
        ],
        compiler_params=remote_params(0),
        name="layer",
    )(rows, cols, features, masks, weight, deg, cotangent)
    return pl.pallas_call(
        hand_on_kernel,
        out_shape=outs,
        in_specs=[spec()] * 3,
        out_specs=(spec(), spec(), spec()),
        name="results",
    )(*results)


def solution(mesh):
    in_specs = (
        P(("col", "row"), None),
        P(),
        P(),
        P("row", "col", None),
        P("row", "col", None),
        P("row", "col", None, None, None),
        P(("row", "col"), None),
    )
    out_specs = (P(("row", "col"), None), P(("col", "row"), None), P())
    return jax.shard_map(body, mesh=mesh, in_specs=in_specs, out_specs=out_specs, check_vma=False)
```

```python
import functools

import jax
import jax.numpy as jnp
from jax import lax
from jax.experimental import pallas as pl
from jax.experimental.pallas import tpu as pltpu
from jax.sharding import PartitionSpec as P

F32 = jnp.float32
BF16 = jnp.bfloat16
I32 = jnp.int32
MESH = pl.DeviceIdType.MESH
VMEM = pltpu.VMEM
SLOTS = 1024
ROW_BITS = 5
COL_BITS = 6
CODE_BITS = ROW_BITS + COL_BITS
FRESH = 24
GROUP = 4
FWD_ROUNDS, FWD_UNROLL = 4, 54
BWD_ROUNDS, BWD_UNROLL = 4, 60
EMPTY = BWD_ROUNDS * BWD_UNROLL
BIG = 56 * 1024 * 1024


def mm(a, b):
    return jnp.dot(a, b, preferred_element_type=F32)


def iota(shape, dim):
    return lax.broadcasted_iota(I32, shape, dim)


def split(x):
    hi = x.astype(BF16)
    return hi, (x - hi.astype(F32)).astype(BF16)


class Place:
    def __init__(self, axis):
        self.axis = axis
        me = lax.axis_index(axis)
        if axis == "row":
            self.core = lax.rem(me, 2)
            chip = me // 2
        else:
            self.core = None
            chip = me
        self.p, self.q = chip // 4, lax.rem(chip, 4)

    def chip(self, name):
        p = 1 - self.p if name[0] == "x" else self.p
        turn = {"": 0, "m": 3, "p": 1, "2": 2}[name[1:]]
        return p * 4 + lax.rem(self.q + turn, 4)

    def index(self, name):
        chip = self.chip(name)
        return chip if self.core is None else chip * 2 + self.core

    def device(self, name):
        if name == "twin":
            return {self.axis: (self.p * 4 + self.q) * 2 + 1 - self.core}
        return {self.axis: self.index(name)}

    def partners(self):
        return ["x", "om", "op"] + ([] if self.core is None else ["twin"])


def send(src, dst, sems, i, device):
    copy = pltpu.make_async_remote_copy(
        src_ref=src,
        dst_ref=dst,
        send_sem=sems[0].at[i],
        recv_sem=sems[1].at[i],
        device_id=device,
        device_id_type=MESH,
    )
    copy.start()
    return copy


def landed(ref, sem):
    pltpu.make_async_copy(ref, ref, sem).wait()


class Place:
    def __init__(self, axis):
        self.axis = axis
        me = lax.axis_index(axis)
        if axis == "row":
            self.core = lax.rem(me, 2)
            chip = me // 2
        else:
            self.core = None
            chip = me
        self.p, self.q = chip // 4, lax.rem(chip, 4)

    def chip(self, name):
        p = 1 - self.p if name[0] == "x" else self.p
        turn = {"": 0, "m": 3, "p": 1, "2": 2}[name[1:]]
        return p * 4 + lax.rem(self.q + turn, 4)

    def index(self, name):
        chip = self.chip(name)
        return chip if self.core is None else chip * 2 + self.core

    def device(self, name):
        if name == "twin":
            return {self.axis: (self.p * 4 + self.q) * 2 + 1 - self.core}
        return {self.axis: self.index(name)}

def send(src, dst, sems, i, device):
    copy = pltpu.make_async_remote_copy(
        src_ref=src,
        dst_ref=dst,
        send_sem=sems[0].at[i],
        recv_sem=sems[1].at[i],
        device_id=device,
        device_id_type=MESH,
    )
    copy.start()
    return copy


def landed(ref, sem):
    pltpu.make_async_copy(ref, ref, sem).wait()


NAMES = ["x", "om", "op", "o2", "xm", "xp", "x2"]


ROUTES = (("x", "op"), ("x", "om"))
SOURCE = {"x": "o2", "op": "xm", "om": "xp"}


def together(*parts):
    for steps in zip(*parts):
        pass


def spread_start(place, mine, out, sems, twin_sems, chunk, sent):
    own = mine.at[pl.ds(2 * chunk, 2)]
    here = out.at[pl.ds(place.index("o") * 4 + 2 * chunk, 2)]
    for i, to in ((1, "op"), (2, "om"), (0, "x")):
        sent.append(send(own, here, sems, 8 * chunk + i, place.device(to)))
    if place.core is not None:
        sent.append(send(own, here, twin_sems, 8 * chunk + 7, place.device("twin")))


def spread(place, out, sems, twin_sems, chunk, sent):
    low = 8 * chunk

    def part(index, first=0, tiles=2):
        return out.at[pl.ds(index * 4 + 2 * chunk + first, tiles)]

    def wait(i, name, first=0, tiles=2):
        landed(part(place.index(name), first, tiles), sems[1].at[low + i])

    def pass_on(i, to, name, first=0, tiles=2):
        ref = part(place.index(name), first, tiles)
        sent.append(send(ref, ref, sems, low + i, place.device(to)))

    def twin(*names):
        if place.core is not None:
            for name in names:
                ref = part(place.index(name))
                i = low + NAMES.index(name)
                sent.append(send(ref, ref, twin_sems, i, place.device("twin")))

    wait(0, "x")
    pass_on(3, "op", "x")
    wait(2, "op")
    pass_on(4, "x", "op")
    pass_on(5, "om", "op")
    yield
    for t, to in reversed(list(enumerate(ROUTES[chunk]))):
        name = SOURCE[to]
        wait({"xm": 3, "xp": 4, "o2": 5}[name], name)
        pass_on(6 + t, to, name, t, 1)
    yield
    wait(1, "om")
    wait(*((4, "xp") if chunk == 0 else (3, "xm")))
    for t in range(2):
        wait(6 + t, "x2", t, 1)
    twin("x", "op", "om", "xm", "xp", "o2", "x2")
    yield
    if place.core is not None:
        for i, name in enumerate(NAMES + ["o"]):
            index = place.chip(name) * 2 + 1 - place.core
            landed(part(index), twin_sems[1].at[low + i])
    yield


def gather_up(place, ready, value, staged, got, sems, chunk, sent):
    low = 8 * chunk
    both = (2 * chunk, 2 * chunk + 1)

    def go(i, slot, into, to, tiles=both):
        at = pl.ds(tiles[0], len(tiles))
        sent.append(send(staged.at[slot, at], got.at[into, at], sems, low + i, place.device(to)))

    def wait(i, into, tiles=both):
        landed(got.at[into, pl.ds(tiles[0], len(tiles))], sems[1].at[low + i])

    def stage(name, slot, *added):
        ready(name)
        for t in both:
            total = value(name, t)
            for into, tiles in added:
                if t in tiles:
                    total = total + got[into, t].astype(F32)
            staged[slot, t] = total.astype(BF16)

    stage("x2", 0)
    go(0, 0, 0, "x", both[:1])
    go(1, 0, 0, ("om", "op")[chunk], both[1:])
    yield
    stage("om", 6)
    go(2, 6, 5, "om")
    if chunk == 0:
        stage("xp", 1)
        go(3, 1, 1, "x")
        wait(1, 0, both[1:])
        stage("xm", 2, (0, both[1:]))
        go(4, 2, 2, "om")
    else:
        stage("xm", 2)
        go(4, 2, 2, "om")
        wait(1, 0, both[1:])
        stage("xp", 1, (0, both[1:]))
        go(3, 1, 1, "x")
    wait(0, 0, both[:1])
    stage("o2", 3, (0, both[:1]))
    go(5, 3, 3, "op")
    yield
    wait(4, 2)
    stage("x", 4, (2, both))
    go(6, 4, 4, "x")
    wait(3, 1)
    wait(5, 3)
    stage("op", 5, (1, both), (3, both))
    go(7, 5, 6, "op")
    yield
    ready("o")
    for i, into in ((2, 5), (6, 4), (7, 6)):
        wait(i, into)
    yield


def gathered_tile(value, got, t):
    total = value("o", t)
    for i in (4, 5, 6):
        total = total + got[i, t].astype(F32)
    return total


def order_list(keys, rows, cols, n_keys, group):
    cap = keys.shape[1]
    hot = iota((n_keys, cap), 0) == keys
    hot_f = hot.astype(F32)
    upper = (iota((cap, cap), 0) < iota((cap, cap), 1)).astype(F32).astype(BF16)
    rank = mm(hot_f.astype(BF16), upper)
    count = jnp.sum(hot_f, axis=1, keepdims=True)
    groups = jnp.floor((count + (group - 1)) * (1.0 / group))
    wide = jnp.broadcast_to(groups, (n_keys, 128)).astype(BF16)
    lower = (iota((n_keys, n_keys), 1) < iota((n_keys, n_keys), 0)).astype(F32).astype(BF16)
    base = mm(lower, wide)[:, :1] * group
    pos = jnp.sum(hot_f * (rank + base), axis=0, keepdims=True)
    opens = jnp.sum(hot_f * rank, axis=0, keepdims=True) < 0.5
    place = (iota((SLOTS, cap), 0) == pos.astype(I32)).astype(F32).astype(BF16)
    which = iota((8, cap), 0)
    slot = iota((8, cap), 1)
    vals = jnp.where(
        which == 0,
        slot >> 4,
        jnp.where(
            which == 1,
            slot & 15,
            jnp.where(which == 2, cols, jnp.where(which == 3, rows, jnp.where(which == 4, 1, opens.astype(I32)))),
        ),
    )
    vals = vals.astype(F32).astype(BF16)
    found = lax.dot_general(vals, place, (((1,), (1,)), ((), ())), preferred_element_type=F32)
    f = found.astype(I32)
    code = ((f[0:1] * 16 + f[1:2]) << CODE_BITS) | (f[2:3] << ROW_BITS) | f[3:4]
    code = jnp.where(f[4:5] > 0, code, cap << CODE_BITS)
    code = code | (f[5:6] << FRESH)
    last = jnp.where(groups > 0.5, base * (1.0 / group) + groups - 1.0, 1.0 * EMPTY)
    square = (n_keys, SLOTS)
    last = jnp.sum(jnp.where(iota(square, 0) == iota(square, 1), last, 0.0), axis=0, keepdims=True)
    return jnp.where(iota((8, SLOTS), 0) == 0, code, last.astype(I32))


def scale_sources(feat, deg, mine):
    lane = iota((128, 128), 1)
    perm = (iota((128, 128), 0) == ((lane & 15) * 8 + (lane >> 4))).astype(F32).astype(BF16)
    degrees = mm(deg[...].astype(F32).astype(BF16), perm)
    bucket = iota((1, 128), 1) >> 4
    shrink = jnp.zeros((1, 128), F32)
    for b in range(8):
        shrink = jnp.where(bucket == b, 2.0**-b, shrink)
    inverse = lax.rsqrt(degrees)
    for t in range(4):
        turned = lax.dot_general(
            feat[t * 128 : (t + 1) * 128, :], perm, (((0,), (0,)), ((), ())), preferred_element_type=F32
        )
        factor = inverse[t : t + 1, :] * shrink
        mine[t] = (turned * factor).astype(BF16)
    return [inverse[t : t + 1, :] * shrink for t in range(4)]


def unpack(held, codes):
    words = jnp.concatenate([held[pl.ds(jnp.minimum((k >> CODE_BITS) & 1023, 768), 1)] for k in codes], axis=0)
    parts = [(words & (1 << b)).astype(F32).astype(BF16) for b in range(8)]
    return jnp.concatenate(parts, axis=1)


def entry(codes, key):
    return jnp.clip(codes[1, key], 0, EMPTY)


def run_tiles(start, stop, unroll, codes, product, acc, run):
    def body(i, carry):
        total = acc[...]
        for u in range(unroll):
            at = (i * unroll + u) * GROUP
            code = [codes[0, at + g] for g in range(GROUP)]
            keep = (1 - ((code[0] >> FRESH) & 1)).astype(F32)
            total = total * keep + product(code)
            run[i * unroll + u] = total
        acc[...] = total
        return carry

    lax.fori_loop(start, stop, body, 0)


def main_kernel(
    scale, n_row, n_col, rows_in, cols_in, feat_in, masks, weight_in, degrees_all, cot_in, act_out, out, gw_out,
    rows, cols, feat, weight, cot, act,
    fwd, bwd, fwd_list, bwd_list, out_factor, back_factor, deg_t, deg_s, src, source, held, acc, run, targets, mine, staged_c, got_c, twin_out, from_twin, staged_r, got_r,
    agg_hold, grad_hold, gw, gw_got, gw_row, gw_col, gw_all,
    sa, ra, st, rt, sc, rc, sg, rg, s0, r0, sr, rr, s2, r2, s3, r3, s4, r4, mask_sem, own_sem, deg_sem, list_sem,
):
    row = lax.axis_index("row")
    col = lax.axis_index("col")
    rows_place, cols_place = Place("row"), Place("col")
    load = pltpu.make_async_copy(masks, held.at[pl.ds(0, 768)], mask_sem)
    load.start()
    loads = [
        pltpu.make_async_copy(degrees_all.at[row * n_col + col], deg_t, deg_sem.at[0]),
        pltpu.make_async_copy(degrees_all.at[col * n_row + row], deg_s, deg_sem.at[1]),
    ]
    pairs = ((rows_in, rows), (cols_in, cols), (feat_in, feat), (weight_in, weight), (cot_in, cot))
    for i, (x, y) in enumerate(pairs):
        loads.append(pltpu.make_async_copy(x, y, deg_sem.at[2 + i]))
    for copy in loads:
        copy.start()
    barrier = pltpu.get_barrier_semaphore()

    def row_peer(step):
        return {"row": lax.rem(row + step, n_row)}

    def col_peer(step):
        return {"col": lax.rem(col + step, n_col)}

    for step in range(1, n_row):
        pl.semaphore_signal(barrier, inc=1, device_id=row_peer(step), device_id_type=MESH)
    for step in range(1, n_col):
        pl.semaphore_signal(barrier, inc=1, device_id=col_peer(step), device_id_type=MESH)
    held[768] = jnp.zeros((16, 128), I32)
    run[EMPTY] = jnp.zeros((128, 128), F32)
    for copy in loads:
        copy.wait()
    act_copy = pltpu.make_async_copy(act, act_out, deg_sem.at[7])
    back_factors = scale_sources(feat, deg_s, source)
    own = pltpu.make_async_copy(source, src.at[pl.ds(rows_place.index("o") * 4, 4)], own_sem)
    own.start()
    pl.semaphore_wait(barrier, n_row + n_col - 2)
    sent = []
    for c in range(2):
        spread_start(rows_place, source, src, (sa, ra), (st, rt), c, sent)
    r, c = rows[...], cols[...]
    fwd_list[...] = order_list(r, r, c, 1 << ROW_BITS, GROUP)
    bwd_list[...] = order_list(c, r, c, 1 << COL_BITS, GROUP)
    lists = [
        pltpu.make_async_copy(fwd_list, fwd, list_sem.at[0]),
        pltpu.make_async_copy(bwd_list, bwd, list_sem.at[1]),
    ]
    for copy in lists:
        copy.start()
    inverse = lax.rsqrt(deg_t[...].astype(F32))
    for t in range(4):
        back_factor[t] = jnp.broadcast_to(back_factors[t], (128, 128)).T
        out_factor[t] = jnp.broadcast_to(inverse[t : t + 1, :], (128, 128)).T
    own.wait()
    together(*[spread(rows_place, src, (sa, ra), (st, rt), c, sent) for c in range(2)])
    load.wait()
    for copy in lists:
        copy.wait()

    def forward(code):
        lhs = jnp.concatenate(
            [src[(k >> ROW_BITS) & ((1 << COL_BITS) - 1)] for k in code], axis=1
        )
        return mm(lhs, unpack(held, code).reshape(GROUP * 128, 128))

    acc[...] = jnp.zeros_like(acc)
    run_tiles(0, FWD_ROUNDS, FWD_UNROLL, fwd, forward, acc, run)

    def forward_sum(name, t):
        return run[entry(fwd, cols_place.index(name) * 4 + t)]

    ups = [
        gather_up(cols_place, lambda name: None, forward_sum, staged_c, got_c, (sc, rc), c, sent)
        for c in range(2)
    ]
    for _ in range(3):
        for up in ups:
            next(up)
    w = weight[...]
    for c in range(2):
        next(ups[c])
        for t in (2 * c, 2 * c + 1):
            summed = gathered_tile(forward_sum, got_c, t)
            agg_t = summed * inverse[t : t + 1, :]
            factor = out_factor[t]
            factor = jnp.concatenate([factor, factor], axis=1)
            hi, lo = split(agg_t.T)
            pre = mm(hi, w) + mm(lo, w)
            slope = jnp.where(pre > 0, 1.0, jnp.exp(jnp.minimum(pre, 0.0)))
            here = pl.ds(t * 128, 128)
            act[here, :] = jnp.where(pre > 0, pre, slope - 1.0).astype(BF16)
            grad = cot[here, :].astype(F32) * slope
            agg_hold[t] = agg_t
            grad_hold[t] = grad
            scaled = (grad * factor).astype(BF16)
            mine[t] = lax.dot_general(
                scaled, w, (((1,), (1,)), ((), ())), preferred_element_type=F32
            ).astype(BF16)
        spread_start(cols_place, mine, targets, (sg, rg), None, c, sent)
    own = pltpu.make_async_copy(mine, targets.at[pl.ds(col * 4, 4)], own_sem)
    own.start()
    act_copy.start()
    total = jnp.zeros((128, 256), F32)
    for t in range(4):
        t_hi, t_lo = split(agg_hold[t])
        g_hi, g_lo = split(grad_hold[t])
        total = total + (mm(t_hi, g_hi) + (mm(t_lo, g_hi) + mm(t_hi, g_lo)))
    gw[...] = total * scale
    own.wait()
    together(*[spread(cols_place, targets, (sg, rg), None, c, sent) for c in range(2)])
    weights = [
        send(
            gw.at[pl.ds(lax.rem(row + step, n_row) * 8, 8)],
            gw_got.at[step],
            (s2, r2),
            step,
            row_peer(step),
        )
        for step in range(1, n_row)
    ]

    def backward(code):
        rhs = jnp.concatenate([targets[k & ((1 << ROW_BITS) - 1)] for k in code], axis=0)
        tiles = unpack(held, code)
        return mm(jnp.concatenate([tiles[g] for g in range(GROUP)], axis=1), rhs)

    acc[...] = jnp.zeros_like(acc)
    run_tiles(0, BWD_ROUNDS // 2, BWD_UNROLL, bwd, backward, acc, run)
    for copy in weights:
        copy.wait()
    summed = gw[pl.ds(row * 8, 8), :]
    for step in range(1, n_row):
        summed = summed + gw_got[step]
    gw_row[...] = summed
    gw_col[pl.ds(col, 1)] = summed[None]
    for step in range(1, n_col):
        sent.append(send(gw_row, gw_col.at[col], (s3, r3), step, col_peer(step)))
    run_tiles(BWD_ROUNDS // 2, BWD_ROUNDS, BWD_UNROLL, bwd, backward, acc, run)

    order = ["x2", "om", "xp", "xm", "o2", "x", "op", "o"]
    for k, name in enumerate(order):
        index = rows_place.chip(name) * 2 + 1 - rows_place.core
        for t in range(4):
            twin_out[k, t] = run[entry(bwd, index * 4 + t)].astype(BF16)
        sent.append(
            send(twin_out.at[k], from_twin.at[k], (s0, r0), k, rows_place.device("twin"))
        )
    arrived = set()

    def ready(name):
        if name not in arrived:
            k = order.index(name)
            landed(from_twin.at[k], r0.at[k])
            arrived.add(name)

    def backward_sum(name, t):
        mine_sum = run[entry(bwd, rows_place.index(name) * 4 + t)]
        return mine_sum + from_twin[order.index(name), t].astype(F32)

    ups = [
        gather_up(rows_place, ready, backward_sum, staged_r, got_r, (sr, rr), c, sent)
        for c in range(2)
    ]
    for up in ups:
        next(up)
    for step in range(1, n_col):
        landed(gw_col.at[lax.rem(col + n_col - step, n_col)], r3.at[step])
    summed = gw_col[0]
    for c in range(1, n_col):
        summed = summed + gw_col[c]
    gw_mine = gw_all.at[pl.ds(row * 8, 8)]
    gw_all[pl.ds(row * 8, 8), :] = summed
    weights = [send(gw_mine, gw_mine, (s4, r4), step, row_peer(step)) for step in range(1, n_row)]
    for _ in range(2):
        for up in ups:
            next(up)
    for t in range(4):
        if t % 2 == 0:
            next(ups[t // 2])
        summed = gathered_tile(backward_sum, got_r, t) * back_factor[t]
        for b in range(8):
            out[pl.ds(t * 128 + b, 16, stride=8), :] = summed[b * 16 : (b + 1) * 16, :]
    for copy in sent:
        copy.wait_send()
    for copy in weights:
        copy.wait_send()
    for step in range(1, n_row):
        peer = lax.rem(row + n_row - step, n_row)
        landed(gw_all.at[pl.ds(peer * 8, 8)], r4.at[step])
    act_copy.wait()
    gw_out[...] = gw_all[...]


def hand_on_kernel(a, b, c, a_out, b_out, c_out):
    a_out[...] = a[...]
    b_out[...] = b[...]
    c_out[...] = c[...]


def spec(space=VMEM):
    return pl.BlockSpec(memory_space=space)


def shaped(shape, dtype):
    return jax.ShapeDtypeStruct(shape, dtype)


def remote_params(number):
    return pltpu.CompilerParams(
        collective_id=number, has_side_effects=True, vmem_limit_bytes=BIG
    )


def dma(count):
    return pltpu.SemaphoreType.DMA((count,))


def body(features, weight, degrees, tile_rows, tile_cols, tile_masks, cotangent):
    n_row = lax.axis_size("row")
    n_col = lax.axis_size("col")
    deg = degrees.reshape(n_row * n_col, 4, 128)
    rows = tile_rows.reshape(1, -1)
    cols = tile_cols.reshape(1, -1)
    masks = tile_masks.reshape(-1, 16, 128)
    hbm = spec(pl.ANY)
    n_rt, n_ct = 4 * n_col, 4 * n_row

    outs = (
        shaped((512, 256), BF16),
        shaped((512, 128), F32),
        shaped((128, 256), F32),
    )
    block = (4, 128, 128)
    results = pl.pallas_call(
        functools.partial(main_kernel, (512 * n_row * n_col) ** -0.5, n_row, n_col),
        out_shape=outs,
        in_specs=[hbm] * 7,
        out_specs=(hbm, spec(), spec()),
        scratch_shapes=[
            VMEM(rows.shape, I32),
            VMEM(cols.shape, I32),
            VMEM(features.shape, BF16),
            VMEM(weight.shape, BF16),
            VMEM(cotangent.shape, BF16),
            VMEM(cotangent.shape, BF16),
            pltpu.SMEM((8, SLOTS), I32),
            pltpu.SMEM((8, SLOTS), I32),
            VMEM((8, SLOTS), I32),
            VMEM((8, SLOTS), I32),
            VMEM(block, F32),
            VMEM(block, F32),
            VMEM((4, 128), I32),
            VMEM((4, 128), I32),
            VMEM((n_ct, 128, 128), BF16),
            VMEM(block, BF16),
            VMEM((776, 16, 128), I32),
            VMEM((128, 128), F32),
            VMEM((EMPTY + 8, 128, 128), F32),
            VMEM((n_rt, 128, 128), BF16),
            VMEM(block, BF16),
            VMEM((7,) + block, BF16),
            VMEM((7,) + block, BF16),
            VMEM((8,) + block, BF16),
            VMEM((8,) + block, BF16),
            VMEM((7,) + block, BF16),
            VMEM((7,) + block, BF16),
            VMEM(block, F32),
            VMEM((4, 128, 256), F32),
            VMEM((128, 256), F32),
            VMEM((n_row, 8, 256), F32),
            VMEM((8, 256), F32),
            VMEM((n_col, 8, 256), F32),
            VMEM((128, 256), F32),
            dma(16),
            dma(16),
            dma(16),
            dma(16),
            dma(16),
            dma(16),
            dma(16),
            dma(16),
            dma(8),
            dma(8),
            dma(16),
            dma(16),
            dma(n_row),
            dma(n_row),
            dma(n_col),
            dma(n_col),
            dma(n_row),
            dma(n_row),
            pltpu.SemaphoreType.DMA,
            pltpu.SemaphoreType.DMA,
            dma(8),
            dma(2),
        ],
        compiler_params=remote_params(0),
        name="layer",
    )(rows, cols, features, masks, weight, deg, cotangent)
    return pl.pallas_call(
        hand_on_kernel,
        out_shape=outs,
        in_specs=[spec()] * 3,
        out_specs=(spec(), spec(), spec()),
        name="results",
    )(*results)


def solution(mesh):
    in_specs = (
        P(("col", "row"), None),
        P(),
        P(),
        P("row", "col", None),
        P("row", "col", None),
        P("row", "col", None, None, None),
        P(("row", "col"), None),
    )
    out_specs = (P(("row", "col"), None), P(("col", "row"), None), P())
    return jax.shard_map(body, mesh=mesh, in_specs=in_specs, out_specs=out_specs, check_vma=False)
```
